512 devices in a mesh: gx: 16 (over x, y_hi), gy: 32 (over z, y_lo, core).
Axes of the slice: x: 4, y: 8 (y_hi: 4, y_lo: 2; y = y_hi * 2 + y_lo), z: 8, core: 2. Of those that a mesh axis runs over, the one named last changes fastest.
Arguments:
- features: bfloat16 [128, 128, 18, 512], P('gx', 'gy'), may hold values from -6 to 6
- mode_weights: bfloat16 [64, 24, 2, 18, 18, 24], P('gy'), may hold values from -0.75 to 0.75
- point_weight: bfloat16 [18, 18], replicated, may hold values from -1.5 to 1.5
- bias_term: float32 [18], replicated, may hold values from -4 to 4
- conv_weight: bfloat16 [27, 18, 18], replicated, may hold values from -0.5 to 0.5
Outputs:
- updated: bfloat16 [128, 128, 18, 512], P('gx', 'gy')
The draws below stay inside these ranges and needn't reach their ends.
All inputs are finite; a program needn't handle non-finite values.
Results may differ from the reference program's by a relative error of at most 0.0085.
Values may be sent and summed in bfloat16 or wider, within the bound.
A program may use at most 128 MiB of HBM per device.

```python
import math
import jax
import jax.numpy as jnp
from jax import lax

GRID_Z = 64
STEPS = 8
CH = 18
MX = 24
MY = 24
MZ = 16
MT = 4
GRID_X = 128
GRID_Y = 128
MODES = 64
DEPTH = 512


def level_of(stream_key, dims, split, low, largest):
    gain = 1.0
    for axis_at, parts in split:
        heights = jax.random.uniform(jax.random.fold_in(jax.random.fold_in(stream_key, 6), axis_at), (parts,), jnp.float32, low / len(split), largest / len(split))
        gain = gain * jnp.repeat(jnp.exp(heights), dims[axis_at] // parts).reshape((-1,) + (1,) * (len(dims) - 1 - axis_at))
    return gain


def scatter_about(stream_key, extent, spread, bound, pieces=(), held_as=jnp.bfloat16):
    drawn = jax.random.normal(stream_key, extent, jnp.float32) * spread
    if len(pieces) > 0:
        drawn = level_of(stream_key, extent, pieces, -0.22, 0.18) * drawn
    return jnp.clip(drawn, min=-bound, max=bound).astype(held_as)


def setup_inputs(seed: int = 0) -> dict:
    streams_of = jax.random.split(jax.random.key(seed), 6)
    features = scatter_about(streams_of[0], (GRID_X, GRID_Y, CH, DEPTH), 1.0, 6.0, ((0, 16), (1, 32)))
    mode_weights = scatter_about(streams_of[1], (MODES, MY, 2, CH, CH, MX), (4 * CH) ** -0.5, 0.75, ((0, 32),))
    point_weight = scatter_about(streams_of[2], (CH, CH), CH ** -0.5, 1.5)
    bias_term = scatter_about(streams_of[3], (CH,), 1.0, 4.0, (), jnp.float32)
    conv_weight = scatter_about(streams_of[4], (27, CH, CH), (27 * CH // 4) ** -0.5, 0.5)
    return dict(features=features, mode_weights=mode_weights, point_weight=point_weight, bias_term=bias_term, conv_weight=conv_weight)


def frequencies(number):
    places = jnp.arange(number, dtype=jnp.int32)
    return jnp.where(places < number // 2, places, places - number)

def phase_angles(number, positions, length):
    fraction = jnp.mod(frequencies(number)[:, None] * positions[None, :], length).astype(jnp.float32) / length
    return 2.0 * math.pi * fraction

def forward_table(number, positions, length):
    angles = phase_angles(number, positions, length).T
    cosine = jnp.cos(angles) / math.sqrt(length)
    sine_part = jnp.sin(angles) / math.sqrt(length)
    return jnp.stack([jnp.stack([cosine, -sine_part], 1), jnp.stack([sine_part, cosine], 1)], 0).astype(jnp.bfloat16)

def inverse_table(number, positions, length):
    angles = phase_angles(number, positions, length)
    cosine = jnp.cos(angles) / math.sqrt(number)
    sine_part = jnp.sin(angles) / math.sqrt(number)
    return jnp.stack([jnp.stack([cosine, sine_part], 1), jnp.stack([-sine_part, cosine], 1)], 0).astype(jnp.bfloat16)

def depth_tables(grid_z, steps, modes_z, modes_t):
    along_z = phase_angles(modes_z, jnp.arange(grid_z, dtype=jnp.int32), grid_z)
    time_freq = jnp.arange(modes_t, dtype=jnp.int32)
    time_pos = jnp.arange(steps, dtype=jnp.int32)
    along_t = 2.0 * math.pi * jnp.mod(time_freq[:, None] * time_pos[None, :], steps).astype(jnp.float32) / steps
    angles = along_z[:, None, :, None] + along_t[None, :, None, :]
    cosine = jnp.cos(angles)
    sine_part = jnp.sin(angles)
    forward = jnp.stack([cosine, -sine_part], 2) / math.sqrt(grid_z * steps)
    forward = forward.reshape(2 * modes_z * modes_t, grid_z * steps).T.astype(jnp.bfloat16)
    factor = jnp.where(time_freq == 0, 1.0, 2.0).astype(jnp.float32)[None, :, None, None] / math.sqrt(modes_z * modes_t)
    inverse = jnp.stack([factor * cosine, -factor * sine_part], 2)
    inverse = inverse.reshape(2 * modes_z * modes_t, grid_z * steps).astype(jnp.bfloat16)
    return (forward, inverse)

def reference(features, mode_weights, point_weight, bias_term, conv_weight):
    flt = jnp.float32
    depth = GRID_Z * STEPS
    zt_forward, zt_inverse = depth_tables(GRID_Z, STEPS, MZ, MT)
    forward_wide = zt_forward.astype(flt)

    def first_row(row_data):
        product = jnp.dot(row_data.reshape(GRID_Y * CH, depth).astype(flt), forward_wide)
        return product.reshape(GRID_Y, CH, 2 * MODES).astype(jnp.bfloat16)
    hat_one = lax.map(first_row, features)
    y_forward = forward_table(MY, jnp.arange(GRID_Y, dtype=jnp.int32), GRID_Y).astype(flt)
    shaped = hat_one.astype(flt).reshape(GRID_X, GRID_Y, CH, MODES, 2)
    hat_two = jnp.einsum('xycmr,rysk->mkscx', shaped, y_forward).astype(jnp.bfloat16)
    x_forward = forward_table(MX, jnp.arange(GRID_X, dtype=jnp.int32), GRID_X).astype(flt)
    hat_three = jnp.einsum('mkrcx,rxsj->mkscj', hat_two.astype(flt), x_forward)
    highest = lax.Precision.HIGHEST
    weights_wide = mode_weights.astype(flt)

    def contract(weight_part, value_part):
        return jnp.einsum('mkcoj,mkcj->mkoj', weight_part, value_part, precision=highest)
    real_part = contract(weights_wide[:, :, 0], hat_three[:, :, 0]) - contract(weights_wide[:, :, 1], hat_three[:, :, 1])
    imag_part = contract(weights_wide[:, :, 0], hat_three[:, :, 1]) + contract(weights_wide[:, :, 1], hat_three[:, :, 0])
    mixed_modes = jnp.stack([real_part, imag_part], 2).astype(jnp.bfloat16)
    x_inverse = inverse_table(MX, jnp.arange(GRID_X, dtype=jnp.int32), GRID_X).astype(flt)
    back_three = jnp.einsum('mkrcj,rjsx->mkscx', mixed_modes.astype(flt), x_inverse).astype(jnp.bfloat16)
    y_inverse = inverse_table(MY, jnp.arange(GRID_Y, dtype=jnp.int32), GRID_Y).astype(flt)
    back_two = jnp.einsum('mkrcx,rksy->msxcy', back_three.astype(flt), y_inverse).astype(jnp.bfloat16)
    back_two = back_two.reshape(2 * MODES, GRID_X, CH, GRID_Y)
    half_y = GRID_Y // 2
    half_depth = depth // 2

    def pool_row(row_pair):
        blocks = row_pair.astype(flt).reshape(2, half_y, 2, CH, GRID_Z // 2, 2, STEPS)
        return blocks.mean(axis=(0, 2, 5)).reshape(half_y, CH, half_depth).astype(jnp.bfloat16)
    pooled = lax.map(pool_row, features.reshape(GRID_X // 2, 2, GRID_Y, CH, depth))
    padded = jnp.pad(pooled.astype(flt), ((1, 1), (1, 1), (0, 0), (STEPS, STEPS)))
    kernel = conv_weight.astype(flt)

    def conv_row(coarse_index):
        window = lax.dynamic_slice_in_dim(padded, coarse_index, 3, 0)
        summed = jnp.zeros((half_y, CH, half_depth), flt)
        for offset in range(27):
            move_x = offset // 9
            move_y = offset // 3 % 3
            move_z = offset % 3
            portion = window[move_x, move_y:move_y + half_y, :, move_z * STEPS:move_z * STEPS + half_depth]
            summed = summed + jnp.einsum('ycs,co->yos', portion, kernel[offset])
        return jax.nn.gelu(summed)
    coarse = lax.map(conv_row, jnp.arange(GRID_X // 2, dtype=jnp.int32))
    zt_back = zt_inverse.astype(flt)
    point = point_weight.astype(flt)

    def out_row(row_index):
        spectral_in = lax.dynamic_index_in_dim(back_two, row_index, 1, False).astype(flt)
        spectral = jnp.einsum('qcy,qs->ycs', spectral_in, zt_back)
        row_data = lax.dynamic_index_in_dim(features, row_index, 0, False).astype(flt)
        pointwise = jnp.einsum('ycs,co->yos', row_data, point)
        coarse_row = lax.dynamic_index_in_dim(coarse, row_index // 2, 0, False).reshape(half_y, CH, GRID_Z // 2, STEPS)
        upsampled = jnp.repeat(jnp.repeat(coarse_row, 2, axis=0), 2, axis=2).reshape(GRID_Y, CH, depth)
        return jax.nn.gelu(spectral + upsampled + pointwise + bias_term[None, :, None]).astype(jnp.bfloat16)
    return lax.map(out_row, jnp.arange(GRID_X, dtype=jnp.int32))
```

```python
import math

import jax
import jax.numpy as jnp
import ml_dtypes
import numpy as np
from jax import lax
from jax.experimental import pallas as pl
from jax.experimental.pallas import tpu as pltpu
from jax.sharding import PartitionSpec as P

BF = jnp.bfloat16
FLT = jnp.float32
MESH = pl.DeviceIdType.MESH

GRID_Z, STEPS, CH = 64, 8, 18
MX, MY, MZ, MT = 24, 24, 16, 4
GX, GY = 16, 32
LX, LY = 8, 4
ROWS = LX * CH * LY
PAIR = 2 * CH * LY
DEPTH = GRID_Z * STEPS
HALF = DEPTH // 2
MODES = MZ * MT
JS = 8
SLOT = 32


def frequencies(number):
    places = np.arange(number, dtype=np.int32)
    return np.where(places < number // 2, places, places - number)


def angles_of(number, length):
    places = np.arange(length, dtype=np.int32)
    fraction = np.mod(frequencies(number)[:, None] * places[None, :], length).astype(np.float32)
    return np.float32(2.0 * math.pi) * (fraction / np.float32(length))


def rounded(table):
    return np.asarray(table, np.float32).astype(ml_dtypes.bfloat16).astype(np.float32)


def forward_table(number, length):
    angles = angles_of(number, length).T
    cosine = np.cos(angles) / np.float32(math.sqrt(length))
    sine = np.sin(angles) / np.float32(math.sqrt(length))
    return rounded(np.stack([np.stack([cosine, -sine], 1), np.stack([sine, cosine], 1)], 0))


def inverse_table(number, length):
    angles = angles_of(number, length)
    cosine = np.cos(angles) / np.float32(math.sqrt(number))
    sine = np.sin(angles) / np.float32(math.sqrt(number))
    return rounded(np.stack([np.stack([cosine, sine], 1), np.stack([-sine, cosine], 1)], 0))


def depth_tables():
    along_z = angles_of(MZ, GRID_Z)
    time_freq = np.arange(MT, dtype=np.int32)
    time_pos = np.arange(STEPS, dtype=np.int32)
    along_t = np.mod(time_freq[:, None] * time_pos[None, :], STEPS).astype(np.float32)
    along_t = np.float32(2.0 * math.pi) * along_t / np.float32(STEPS)
    angles = along_z[:, None, :, None] + along_t[None, :, None, :]
    cosine, sine = np.cos(angles), np.sin(angles)
    forward = np.stack([cosine, -sine], 2) / np.float32(math.sqrt(DEPTH))
    forward = forward.reshape(2 * MODES, DEPTH)
    factor = np.where(time_freq == 0, 1.0, 2.0).astype(np.float32)[None, :, None, None]
    factor = factor / np.float32(math.sqrt(MODES))
    inverse = np.stack([factor * cosine, -factor * sine], 2).reshape(2 * MODES, DEPTH)
    return rounded(forward), rounded(inverse)


def make_tables():
    zt_forward, zt_inverse = depth_tables()
    yf, yi = forward_table(MY, GY * LY), inverse_table(MY, GY * LY)
    xf, xi = forward_table(MX, GX * LX), inverse_table(MX, GX * LX)
    eye2 = np.eye(2, dtype=np.float32)
    per = MY // 8
    block = yf.reshape(2, GY, LY, 2, 8, per)
    ty = np.zeros((LY, 2, 8, JS, GY, 2, 2), np.float32)
    ty[:, :, :, : 2 * per] = np.einsum("rgysaj,mn->ymajsgnr", block, eye2).reshape(
        LY, 2, 8, 2 * per, GY, 2, 2
    )
    ty = ty.reshape(LY * GX * JS, GY * 4)
    eyex, eyec, eyey = np.eye(LX), np.eye(CH, SLOT), np.eye(LY)
    gather = np.einsum("xX,cC,y->xcyXC", eyex, eyec, np.ones(LY)).reshape(ROWS, LX * SLOT)
    block = xf.reshape(2, GX, 2, 4, 2, MX)
    eyej = np.eye(per)
    tx = np.zeros((GX, 2, JS, per, 2, 4, SLOT), np.float32)
    tx[:, :, : 2 * per, :, :, :, :MX] = np.einsum("rahusk,ij->ahirjsuk", block, eyej).reshape(
        GX, 2, 2 * per, per, 2, 4, MX
    )
    tx = tx.reshape(GX * 2 * JS, per * 2 * 4 * SLOT)
    block = xi.reshape(2, MX, 2, GX, 2, 4)
    tix = np.zeros((GX, 2, JS, per, 2, 4, SLOT), np.float32)
    tix[:, :, : 2 * per, :, :, :, :MX] = np.einsum("rksahu,ij->ahisjruk", block, eyej).reshape(
        GX, 2, 2 * per, per, 2, 4, MX
    )
    tix = tix.reshape(GX * 2 * JS, per * 2 * 4 * SLOT)
    block = yi.reshape(2, 8, per, 2, GY, LY)
    tiy = np.zeros((LY, GY, 2, 2, 2, 8, JS), np.float32)
    tiy[..., : 2 * per] = np.einsum("rajsgy,mn->ygmsnajr", block, eye2).reshape(
        LY, GY, 2, 2, 2, 8, 2 * per
    )
    tiy = tiy.reshape(LY * GY * 4, GX * JS)
    pair_pool = np.einsum("x,cC,yY->YCxcy", np.ones(2), np.eye(CH), np.repeat(np.eye(2), 2, 0))
    pair_pool = pair_pool.reshape(2 * CH, PAIR)
    lane_up = np.einsum("zZ,tT->ZTzt", np.repeat(np.eye(GRID_Z // 2), 2, 0), np.eye(STEPS))
    lane_up = lane_up.reshape(HALF, DEPTH)
    lane_pool = 0.125 * lane_up.T
    row_up = np.zeros((PAIR, 40), np.float32)
    row_up[:, : 2 * CH] = pair_pool.T
    spread_o = np.einsum("x,oO,y->xoyO", np.ones(2), np.eye(CH), np.ones(LY)).reshape(PAIR, CH)
    same = np.einsum("xX,oc,yY->xoyXcY", np.eye(2), np.ones((CH, CH)), eyey).reshape(PAIR, PAIR)
    conv_rows = np.zeros((2, 3, 40, 3, CH), np.float32)
    conv_lanes = np.zeros((2, 3, 3, CH, 3, 4, CH), np.float32)
    for at in range(2):
        for dz in range(3):
            conv_rows[at, dz, at * CH : (at + 1) * CH, dz] = np.eye(CH)
        for dx in range(3):
            for dy in range(3):
                conv_lanes[at, dx, dy, :, dx, dy + at] = np.eye(CH)
    conv_rows = conv_rows.reshape(2, 120, 3 * CH)
    conv_lanes = conv_lanes.reshape(2, 9 * CH, 12 * CH)
    return [
        np.asarray(t, np.float32).astype(ml_dtypes.bfloat16)
        for t in (
            zt_forward,
            ty,
            gather,
            tx,
            tix,
            gather.T,
            tiy,
            zt_inverse,
            pair_pool,
            lane_pool,
            lane_up,
            row_up,
            spread_o,
            same,
            conv_rows,
            conv_lanes,
        )
    ]


def mm(a, b):
    return jnp.dot(a, b, preferred_element_type=FLT)


def mm_nt(a, b):
    return lax.dot_general(a, b, (((1,), (1,)), ((), ())), preferred_element_type=FLT)


def mm_tn(a, b):
    return lax.dot_general(a, b, (((0,), (0,)), ((), ())), preferred_element_type=FLT)


def halves(value):
    high = value.astype(BF)
    return high, (value - high.astype(FLT)).astype(BF)


def kernel(*refs):
    (f_hbm, w_hbm, pw_hbm, bias_hbm, cw_hbm), refs = refs[:5], refs[5:]
    tables_hbm, refs = refs[:16], refs[16:]
    out_hbm, refs = refs[0], refs[1:]
    (f_in, w_in, pw_in, bias_in, cw_in), refs = refs[:5], refs[5:]
    tables, refs = refs[:16], refs[16:]
    (
        f_rows,
        send_one,
        recv_one,
        send_two,
        recv_two,
        send_three,
        recv_three,
        send_four,
        recv_four,
        pool,
        point,
        conv,
        w_wide,
        third,
        mixed,
        base,
        out_rows,
        in_sem,
        table_sem,
        send_sem,
        recv_sem,
        own_sem,
        halo_send,
        halo_recv,
        out_sem,
    ) = refs
    (
        t_zf,
        t_y,
        t_gather,
        t_x,
        t_ix,
        t_spread,
        t_iy,
        t_zi,
        t_pair_pool,
        t_lane_pool,
        t_lane_up,
        t_row_up,
        t_spread_o,
        t_same,
        t_conv_rows,
        t_conv_lanes,
    ) = tables
    gx = lax.axis_index("gx")
    gy = lax.axis_index("gy")
    barrier = pltpu.get_barrier_semaphore()

    def on_gx(step):
        return (lax.rem(gx + step, GX), gy)

    def on_gy(step):
        return (gx, lax.rem(gy + step, GY))

    def greet(target):
        pl.semaphore_signal(barrier, inc=1, device_id=target, device_id_type=MESH)

    mine = [
        pltpu.make_async_copy(f_hbm, f_in, in_sem.at[0]),
        pltpu.make_async_copy(
            w_hbm.at[gx // 8, pl.ds(3 * lax.rem(gx, 8), 3)], w_in, in_sem.at[1]
        ),
        pltpu.make_async_copy(pw_hbm, pw_in, in_sem.at[2]),
        pltpu.make_async_copy(bias_hbm, bias_in, in_sem.at[3]),
        pltpu.make_async_copy(cw_hbm, cw_in, in_sem.at[4]),
    ]
    loads = [
        pltpu.make_async_copy(tables_hbm[i], tables[i], table_sem.at[i]) for i in range(16)
    ]
    loads[0].start()
    mine[0].start()

    def greet_gy(step, _):
        greet(on_gy(step))
        return 0

    def greet_gx(step, _):
        greet(on_gx(step))
        return 0

    lax.fori_loop(1, GY, greet_gy, 0)
    lax.fori_loop(1, GX, greet_gx, 0)
    sides = [(dx, dy) for dx in (-1, 0, 1) for dy in (-1, 0, 1) if (dx, dy) != (0, 0)]

    def beside(dx, dy):
        return (lax.rem(gx + dx + GX, GX), lax.rem(gy + dy + GY, GY))

    for dx, dy in sides:
        if dx != 0 and dy != 0:
            greet(beside(dx, dy))
    for load in loads[1:]:
        load.start()
    for load in mine[1:]:
        load.start()

    mine[0].wait()
    loads[0].wait()
    f_rows[...] = f_in.reshape(ROWS, DEPTH)[...]
    hat = mm_nt(t_zf[...], f_rows[...]).astype(BF)
    send_one[...] = hat.reshape(GY, 4, ROWS)

    def all_to_all(at, count, source, target, me, place):
        own = pltpu.make_async_copy(source.at[me], target.at[me], own_sem.at[at])
        own.start()

        def send(step, _):
            to = place(step)
            pltpu.make_async_remote_copy(
                src_ref=source.at[to[1] if count == GY else to[0]],
                dst_ref=target.at[me],
                send_sem=send_sem.at[at],
                recv_sem=recv_sem.at[at],
                device_id=to,
                device_id_type=MESH,
            ).start()
            return 0

        lax.fori_loop(1, count, send, 0)

        def arrive():
            own.wait()
            part = target.at[pl.ds(0, count - 1)]
            pltpu.make_async_copy(part, part, recv_sem.at[at]).wait()

        def leave():
            part = source.at[pl.ds(0, count - 1)]
            pltpu.make_async_copy(part, part, send_sem.at[at]).wait()

        return arrive, leave

    pl.semaphore_wait(barrier, (GY - 1) + (GX - 1) + 4)
    arrive_one, leave_one = all_to_all(0, GY, send_one, recv_one, gy, on_gy)

    for i in (8, 9):
        loads[i].wait()
    for pair in range(LX // 2):
        rows = mm(t_pair_pool[...], f_rows[pair * PAIR : (pair + 1) * PAIR])
        high, low = halves(rows)
        cells = mm(high, t_lane_pool[...]) + mm(low, t_lane_pool[...])
        pool[pair + 1, 1:3] = cells.astype(BF).reshape(2, 9, 2, HALF)

    def rim(which, dx, dy):
        sx = {-1: pl.ds(1, 1), 0: pl.ds(1, 4), 1: pl.ds(4, 1)}[dx]
        tx = {-1: pl.ds(5, 1), 0: pl.ds(1, 4), 1: pl.ds(0, 1)}[dx]
        sy = {-1: pl.ds(1, 1), 0: pl.ds(1, 2), 1: pl.ds(2, 1)}[dy]
        ty = {-1: pl.ds(3, 1), 0: pl.ds(1, 2), 1: pl.ds(0, 1)}[dy]
        return pltpu.make_async_remote_copy(
            src_ref=pool.at[sx, sy],
            dst_ref=pool.at[tx, ty],
            send_sem=halo_send.at[which],
            recv_sem=halo_recv.at[which],
            device_id=beside(dx, dy),
            device_id_type=MESH,
        )

    rims = [rim(i, dx, dy) for i, (dx, dy) in enumerate(sides)]
    for copy in rims:
        copy.start()

    for i in range(1, 5):
        mine[i].wait()
    for i in range(11, 16):
        loads[i].wait()
    wide = mm_nt(t_spread_o[...], pw_in[...]).astype(BF)
    wide = mm_nt(wide, t_spread_o[...]).astype(BF)
    point[...] = wide * t_same[...]
    conv_sum = jnp.zeros((120, 12 * CH), FLT)
    for at in range(2):
        lanes = mm(cw_in[...], t_conv_lanes[at]).astype(BF)
        conv_sum = conv_sum + mm(t_conv_rows[at], lanes)
    conv[...] = conv_sum.astype(BF)

    def widen(at, _):
        w_wide[at, :, 0:MX] = w_in.reshape(3 * CH, CH, 2, MX)[at].astype(FLT).reshape(2 * CH, MX)
        return 0

    lax.fori_loop(0, 3 * CH, widen, 0)
    mixed[...] = jnp.zeros_like(mixed)

    for i in (1, 2):
        loads[i].wait()
    arrive_one()
    lane = lax.broadcasted_iota(jnp.int32, (GX * JS, ROWS), 1)
    part = mm(t_y[...], recv_one[...].reshape(4 * GY, ROWS)).reshape(LY, GX * JS, ROWS)
    chosen = part[0]
    for y in range(1, LY):
        chosen = jnp.where(lax.rem(lane, LY) == y, part[y], chosen)
    high, low = halves(chosen)
    second = mm(high, t_gather[...]) + mm(low, t_gather[...])
    second = [second[:, h * 128 : (h + 1) * 128].reshape(GX, JS, 128) for h in range(2)]
    send_two[...] = jnp.concatenate(second, axis=1).astype(BF)
    arrive_two, leave_two = all_to_all(1, GX, send_two, recv_two, gx, on_gx)

    for i in (10,):
        loads[i].wait()
    for copy in rims:
        copy.wait_recv()

    @pl.when(gx == 0)
    def _():
        pool[0] = jnp.zeros((4, 9, 2, HALF), BF)

    @pl.when(gx == GX - 1)
    def _():
        pool[5] = jnp.zeros((4, 9, 2, HALF), BF)

    @pl.when(gy == 0)
    def _():
        pool[:, 0] = jnp.zeros((6, 9, 2, HALF), BF)

    @pl.when(gy == GY - 1)
    def _():
        pool[:, 3] = jnp.zeros((6, 9, 2, HALF), BF)

    column = jnp.sum(t_spread_o[...].astype(FLT) * bias_in[...], axis=1, keepdims=True)
    spot = lax.broadcasted_iota(jnp.int32, (40, HALF), 1)
    for pair in range(LX // 2):
        sums = mm(conv[...], pool[pair : pair + 3].reshape(12 * CH, HALF))
        below = jnp.where(spot >= STEPS, pltpu.roll(sums[0:40], STEPS, 1), 0.0)
        above = jnp.where(spot < HALF - STEPS, pltpu.roll(sums[80:120], HALF - STEPS, 1), 0.0)
        high, low = halves(jax.nn.gelu(sums[40:80] + below + above))
        span = slice(pair * PAIR, (pair + 1) * PAIR)
        up = mm(t_row_up[...], mm(high, t_lane_up[...]).astype(BF))
        up = up + mm(t_row_up[...], mm(low, t_lane_up[...]).astype(BF))
        base[span] = mm(point[...], f_rows[span]) + up + column

    for i in (3, 4):
        loads[i].wait()
    arrive_two()
    turned = mm_tn(recv_two[...].reshape(GX * 2 * JS, 128), t_x[...])
    group = lax.broadcasted_iota(jnp.int32, (SLOT, 128), 1) // SLOT
    for at in range(6):
        acc = jnp.zeros((SLOT, 128), FLT)
        for u in range(4):
            piece = turned[u * SLOT : (u + 1) * SLOT, at * 128 : (at + 1) * 128]
            acc = acc + jnp.where(group == u, piece, 0.0)
        acc = acc + pltpu.roll(acc, 64, 1)
        acc = acc + pltpu.roll(acc, 32, 1)
        third[at] = acc

    for j in range(3):
        real = jnp.zeros((CH, 128), FLT)
        imag = jnp.zeros((CH, 128), FLT)
        for c in range(CH):
            w_real = w_wide[j * CH + c, pl.ds(0, CH, stride=2), :]
            w_imag = w_wide[j * CH + c, pl.ds(1, CH, stride=2), :]
            u_real = third[2 * j, c : c + 1, :]
            u_imag = third[2 * j + 1, c : c + 1, :]
            real = real + (w_real * u_real - w_imag * u_imag)
            imag = imag + (w_real * u_imag + w_imag * u_real)
        mixed[2 * j, 0:CH, 0:MX] = real[:, 0:MX]
        mixed[2 * j + 1, 0:CH, 0:MX] = imag[:, 0:MX]

    blocks = []
    for at in range(6):
        value = mixed[at]
        value = value + pltpu.roll(value, 32, 1)
        value = value + pltpu.roll(value, 64, 1)
        tall = [jnp.where(group == u, value, 0.0) for u in range(4)]
        blocks.append(jnp.concatenate(tall, axis=0).astype(BF))
    back = mm_nt(t_ix[...], jnp.concatenate(blocks, axis=1))
    send_three[...] = back.astype(BF).reshape(GX, 2 * JS, 128)
    arrive_three, leave_three = all_to_all(2, GX, send_three, recv_three, gx, on_gx)

    for i in (5, 6, 7):
        loads[i].wait()
    arrive_three()
    wide_in = recv_three[...].astype(FLT)
    sides_in = [wide_in[:, h * JS : (h + 1) * JS].reshape(GX * JS, 128) for h in range(2)]
    spread = mm(jnp.concatenate(sides_in, axis=1).astype(BF), t_spread[...]).astype(BF)
    part = mm(t_iy[...], spread).reshape(LY, 4 * GY, ROWS)
    chosen = part[0]
    for y in range(1, LY):
        chosen = jnp.where(lax.rem(lane, LY) == y, part[y], chosen)
    send_four[...] = chosen.astype(BF).reshape(GY, 4, ROWS)
    arrive_four, leave_four = all_to_all(3, GY, send_four, recv_four, gy, on_gy)

    arrive_four()
    columns = recv_four[...].reshape(4 * GY, ROWS).astype(FLT).T.astype(BF)
    stores = []
    for pair in range(LX // 2):
        span = slice(pair * PAIR, (pair + 1) * PAIR)
        total = mm(columns[span], t_zi[...]) + base[span]
        out_rows[pair * 36 : (pair + 1) * 36] = jax.nn.gelu(total).astype(BF).reshape(36, 4, DEPTH)
        store = pltpu.make_async_copy(
            out_rows.at[pl.ds(pair * 36, 36)],
            out_hbm.at[pl.ds(pair * 36, 36)],
            out_sem.at[pair],
        )
        store.start()
        stores.append(store)
    for leave in (leave_one, leave_two, leave_three, leave_four):
        leave()
    for copy in rims:
        copy.wait_send()
    for store in stores:
        store.wait()


def local(features, mode_weights, point_weight, bias_term, conv_weight):
    tables = make_tables()
    f = features.transpose(0, 2, 1, 3).reshape(LX * CH, LY, DEPTH)
    w = mode_weights.transpose(0, 1, 3, 4, 2, 5)
    taps = conv_weight.reshape(3, 3, 3, CH, CH).transpose(2, 4, 0, 1, 3).reshape(3 * CH, 9 * CH)
    operands = [f, w, point_weight, bias_term.reshape(1, CH), taps]
    vmem = [
        pltpu.VMEM(f.shape, BF),
        pltpu.VMEM((3,) + w.shape[2:], BF),
        pltpu.VMEM(point_weight.shape, BF),
        pltpu.VMEM((1, CH), FLT),
        pltpu.VMEM(taps.shape, BF),
    ]
    vmem += [pltpu.VMEM(t.shape, BF) for t in tables]
    vmem += [
        pltpu.VMEM((ROWS, DEPTH), BF),
        pltpu.VMEM((GY, 4, ROWS), BF),
        pltpu.VMEM((GY, 4, ROWS), BF),
        pltpu.VMEM((GX, 2 * JS, 128), BF),
        pltpu.VMEM((GX, 2 * JS, 128), BF),
        pltpu.VMEM((GX, 2 * JS, 128), BF),
        pltpu.VMEM((GX, 2 * JS, 128), BF),
        pltpu.VMEM((GY, 4, ROWS), BF),
        pltpu.VMEM((GY, 4, ROWS), BF),
        pltpu.VMEM((6, 4, 9, 2, HALF), BF),
        pltpu.VMEM((PAIR, PAIR), BF),
        pltpu.VMEM((120, 12 * CH), BF),
        pltpu.VMEM((3 * CH, 2 * CH, 128), FLT),
        pltpu.VMEM((6, SLOT, 128), FLT),
        pltpu.VMEM((6, SLOT, 128), FLT),
        pltpu.VMEM((ROWS, DEPTH), FLT),
        pltpu.VMEM(f.shape, BF),
        pltpu.SemaphoreType.DMA((5,)),
        pltpu.SemaphoreType.DMA((16,)),
        pltpu.SemaphoreType.DMA((4,)),
        pltpu.SemaphoreType.DMA((4,)),
        pltpu.SemaphoreType.DMA((4,)),
        pltpu.SemaphoreType.DMA((8,)),
        pltpu.SemaphoreType.DMA((8,)),
        pltpu.SemaphoreType.DMA((4,)),
    ]
    out = pl.pallas_call(
        kernel,
        out_shape=jax.ShapeDtypeStruct(f.shape, BF),
        in_specs=[pl.BlockSpec(memory_space=pl.ANY)] * (5 + len(tables)),
        out_specs=pl.BlockSpec(memory_space=pl.ANY),
        scratch_shapes=vmem,
        compiler_params=pltpu.CompilerParams(
            collective_id=0, has_side_effects=True, vmem_limit_bytes=48 << 20
        ),
        name="layer",
    )(*operands, *[jnp.asarray(t) for t in tables])
    return out.reshape(LX, CH, LY, DEPTH).transpose(0, 2, 1, 3)


def solution(mesh):
    in_specs = (P("gx", "gy", None, None), P("gy", None, None, None, None, None), P(), P(), P())
    out_specs = P("gx", "gy", None, None)
    return jax.shard_map(local, mesh=mesh, in_specs=in_specs, out_specs=out_specs, check_vma=False)
```

```python
import math

import jax
import jax.numpy as jnp
import ml_dtypes
import numpy as np
from jax import lax
from jax.experimental import pallas as pl
from jax.experimental.pallas import tpu as pltpu
from jax.sharding import PartitionSpec as P

BF = jnp.bfloat16
FLT = jnp.float32
MESH = pl.DeviceIdType.MESH

GRID_Z, STEPS, CH = 64, 8, 18
MX, MY, MZ, MT = 24, 24, 16, 4
GX, GY = 16, 32
LX, LY = 8, 4
ROWS = LX * CH * LY
PAIR = 2 * CH * LY
DEPTH = GRID_Z * STEPS
HALF = DEPTH // 2
MODES = MZ * MT
JS = 8
SLOT = 32
TABLES = 17


def frequencies(number):
    places = np.arange(number, dtype=np.int32)
    return np.where(places < number // 2, places, places - number)


def angles_of(number, length):
    places = np.arange(length, dtype=np.int32)
    fraction = np.mod(frequencies(number)[:, None] * places[None, :], length).astype(np.float32)
    return np.float32(2.0 * math.pi) * (fraction / np.float32(length))


def rounded(table):
    return np.asarray(table, np.float32).astype(ml_dtypes.bfloat16).astype(np.float32)


def forward_table(number, length):
    angles = angles_of(number, length).T
    cosine = np.cos(angles) / np.float32(math.sqrt(length))
    sine = np.sin(angles) / np.float32(math.sqrt(length))
    return rounded(np.stack([np.stack([cosine, -sine], 1), np.stack([sine, cosine], 1)], 0))


def inverse_table(number, length):
    angles = angles_of(number, length)
    cosine = np.cos(angles) / np.float32(math.sqrt(number))
    sine = np.sin(angles) / np.float32(math.sqrt(number))
    return rounded(np.stack([np.stack([cosine, sine], 1), np.stack([-sine, cosine], 1)], 0))


def depth_tables():
    along_z = angles_of(MZ, GRID_Z)
    time_freq = np.arange(MT, dtype=np.int32)
    time_pos = np.arange(STEPS, dtype=np.int32)
    along_t = np.mod(time_freq[:, None] * time_pos[None, :], STEPS).astype(np.float32)
    along_t = np.float32(2.0 * math.pi) * along_t / np.float32(STEPS)
    angles = along_z[:, None, :, None] + along_t[None, :, None, :]
    cosine, sine = np.cos(angles), np.sin(angles)
    forward = np.stack([cosine, -sine], 2) / np.float32(math.sqrt(DEPTH))
    forward = forward.reshape(2 * MODES, DEPTH)
    factor = np.where(time_freq == 0, 1.0, 2.0).astype(np.float32)[None, :, None, None]
    factor = factor / np.float32(math.sqrt(MODES))
    inverse = np.stack([factor * cosine, -factor * sine], 2).reshape(2 * MODES, DEPTH)
    return rounded(forward), rounded(inverse)


def make_tables():
    zt_forward, zt_inverse = depth_tables()
    yf, yi = forward_table(MY, GY * LY), inverse_table(MY, GY * LY)
    xf, xi = forward_table(MX, GX * LX), inverse_table(MX, GX * LX)
    eye2 = np.eye(2, dtype=np.float32)
    per = MY // 8
    block = yf.reshape(2, GY, LY, 2, 8, per)
    ty = np.zeros((LY, 2, 8, JS, GY, 2, 2), np.float32)
    ty[:, :, :, : 2 * per] = np.einsum("rgysaj,mn->ymajsgnr", block, eye2).reshape(
        LY, 2, 8, 2 * per, GY, 2, 2
    )
    ty = ty.reshape(LY * GX * JS, GY * 4)
    eyex, eyec, eyey = np.eye(LX), np.eye(CH, SLOT), np.eye(LY)
    gather = np.einsum("xX,cC,y->xcyXC", eyex, eyec, np.ones(LY)).reshape(ROWS, LX * SLOT)
    block = xf.reshape(2, GX, 2, 4, 2, MX)
    eyej = np.eye(per)
    tx = np.zeros((GX, 2, JS, per, 2, 4, SLOT), np.float32)
    tx[:, :, : 2 * per, :, :, :, :MX] = np.einsum("rahusk,ij->ahirjsuk", block, eyej).reshape(
        GX, 2, 2 * per, per, 2, 4, MX
    )
    tx = tx.reshape(GX * 2 * JS, per * 2 * 4 * SLOT)
    block = xi.reshape(2, MX, 2, GX, 2, 4)
    tix = np.zeros((GX, 2, JS, per, 2, 4, SLOT), np.float32)
    tix[:, :, : 2 * per, :, :, :, :MX] = np.einsum("rksahu,ij->ahisjruk", block, eyej).reshape(
        GX, 2, 2 * per, per, 2, 4, MX
    )
    tix = tix.reshape(GX * 2 * JS, per * 2 * 4 * SLOT)
    block = yi.reshape(2, 8, per, 2, GY, LY)
    tiy = np.zeros((LY, GY, 2, 2, 2, 8, JS), np.float32)
    tiy[..., : 2 * per] = np.einsum("rajsgy,mn->ygmsnajr", block, eye2).reshape(
        LY, GY, 2, 2, 2, 8, 2 * per
    )
    tiy = tiy.reshape(LY * GY * 4, GX * JS)
    pair_pool = np.einsum("x,cC,yY->YCxcy", np.ones(2), np.eye(CH), np.repeat(np.eye(2), 2, 0))
    pair_pool = pair_pool.reshape(2 * CH, PAIR)
    lane_up = np.einsum("zZ,tT->ZTzt", np.repeat(np.eye(GRID_Z // 2), 2, 0), np.eye(STEPS))
    lane_up = lane_up.reshape(HALF, DEPTH)
    lane_pool = 0.125 * lane_up.T
    row_up = np.zeros((PAIR, 2, 24), np.float32)
    row_up[:, :, :CH] = pair_pool.T.reshape(PAIR, 2, CH)
    row_up = row_up.reshape(PAIR, 48)
    spread_o = np.einsum("x,oO,y->xoyO", np.ones(2), np.eye(CH), np.ones(LY)).reshape(PAIR, CH)
    same = np.einsum("xX,oc,yY->xoyXcY", np.eye(2), np.ones((CH, CH)), eyey).reshape(PAIR, PAIR)
    eyecc = np.eye(CH, dtype=np.float32)
    conv_place = np.zeros((3, 2, 128, 3, 4, CH), np.float32)
    for dx in range(3):
        for dy in range(3):
            for dz in range(3):
                for at in range(2):
                    conv_place[dz, at, 9 * dx + 3 * dy + dz, dx, dy + at] = 1.0
    conv_place = conv_place.reshape(6, 128, 12 * CH)
    conv_same = np.einsum("cC,o,d->coCd", eyecc, np.ones(24), np.ones(12))
    conv_same = conv_same.transpose(0, 1, 3, 2).reshape(24 * CH, 12 * CH)
    conv_sum = np.einsum("c,oO->ocO", np.ones(CH), np.eye(24)).reshape(24, 24 * CH)
    return [
        np.asarray(t, np.float32).astype(ml_dtypes.bfloat16)
        for t in (
            zt_forward,
            ty,
            gather,
            tx,
            tix,
            gather.T,
            tiy,
            zt_inverse,
            pair_pool,
            lane_pool,
            lane_up,
            row_up,
            spread_o,
            same,
            conv_place,
            conv_same,
            conv_sum,
        )
    ]


def mm(a, b):
    return jnp.dot(a, b, preferred_element_type=FLT)


def mm_nt(a, b):
    return lax.dot_general(a, b, (((1,), (1,)), ((), ())), preferred_element_type=FLT)


def mm_tn(a, b):
    return lax.dot_general(a, b, (((0,), (0,)), ((), ())), preferred_element_type=FLT)


def halves(value):
    high = value.astype(BF)
    return high, (value - high.astype(FLT)).astype(BF)


def kernel(*refs):
    (f_hbm, w_hbm, pw_hbm, bias_hbm, cw_hbm), refs = refs[:5], refs[5:]
    tables_hbm, refs = refs[:TABLES], refs[TABLES:]
    out_hbm, refs = refs[0], refs[1:]
    (f_in, w_in, pw_in, bias_in, cw_in), refs = refs[:5], refs[5:]
    tables, refs = refs[:TABLES], refs[TABLES:]
    (
        f_rows,
        send_one,
        recv_one,
        send_two,
        recv_two,
        send_three,
        recv_three,
        send_four,
        recv_four,
        pool,
        point,
        taps,
        conv,
        w_wide,
        third,
        mixed,
        base,
        out_rows,
        in_sem,
        table_sem,
        send_sem,
        recv_sem,
        own_sem,
        halo_send,
        halo_recv,
        out_sem,
    ) = refs
    (
        t_zf,
        t_y,
        t_gather,
        t_x,
        t_ix,
        t_spread,
        t_iy,
        t_zi,
        t_pair_pool,
        t_lane_pool,
        t_lane_up,
        t_row_up,
        t_spread_o,
        t_same,
        t_conv_place,
        t_conv_same,
        t_conv_sum,
    ) = tables
    gx = lax.axis_index("gx")
    gy = lax.axis_index("gy")
    barrier = pltpu.get_barrier_semaphore()

    def far_first(step, count):
        sign = 1 - 2 * lax.rem(step, 2)
        return count // 2 + sign * lax.div(step + 1, 2)

    def on_gx(step):
        x = lax.rem(lax.div(gx, 4) + far_first(lax.rem(step, 4), 4), 4)
        y = lax.rem(lax.rem(gx, 4) + far_first(lax.div(step, 4), 4), 4)
        return (4 * x + y, gy)

    def on_gy(step):
        z = lax.rem(lax.div(gy, 4) + far_first(lax.div(step, 4), 8), 8)
        low = lax.rem(lax.rem(gy, 4) + far_first(lax.rem(step, 4), 4), 4)
        return (gx, 4 * z + low)

    def greet(target):
        pl.semaphore_signal(barrier, inc=1, device_id=target, device_id_type=MESH)

    mine = [
        pltpu.make_async_copy(f_hbm, f_in, in_sem.at[0]),
        pltpu.make_async_copy(
            w_hbm.at[gx // 8, pl.ds(3 * lax.rem(gx, 8), 3)], w_in, in_sem.at[1]
        ),
        pltpu.make_async_copy(pw_hbm, pw_in, in_sem.at[2]),
        pltpu.make_async_copy(bias_hbm, bias_in, in_sem.at[3]),
        pltpu.make_async_copy(cw_hbm, cw_in, in_sem.at[4]),
    ]
    loads = [
        pltpu.make_async_copy(tables_hbm[i], tables[i], table_sem.at[i]) for i in range(TABLES)
    ]
    loads[0].start()
    mine[0].start()

    def greet_gy(step, _):
        greet(on_gy(step))
        return 0

    def greet_gx(step, _):
        greet(on_gx(step))
        return 0

    lax.fori_loop(0, GY - 1, greet_gy, 0)
    lax.fori_loop(0, GX - 1, greet_gx, 0)
    sides = [(dx, dy) for dx in (-1, 0, 1) for dy in (-1, 0, 1) if (dx, dy) != (0, 0)]

    def beside(dx, dy):
        return (lax.rem(gx + dx + GX, GX), lax.rem(gy + dy + GY, GY))

    for dx, dy in sides:
        if dx != 0 and dy != 0:
            greet(beside(dx, dy))
    for load in loads[1:]:
        load.start()
    for load in mine[1:]:
        load.start()

    mine[0].wait()
    loads[0].wait()
    f_rows[...] = f_in.reshape(ROWS, DEPTH)[...]
    hat = mm_nt(t_zf[...], f_rows[...]).astype(BF)
    send_one[...] = hat.reshape(GY, 4, ROWS)

    def all_to_all(at, count, source, target, me, place):
        own = pltpu.make_async_copy(source.at[me], target.at[me], own_sem.at[at])
        own.start()

        def send(step, _):
            to = place(step)
            pltpu.make_async_remote_copy(
                src_ref=source.at[to[1] if count == GY else to[0]],
                dst_ref=target.at[me],
                send_sem=send_sem.at[at],
                recv_sem=recv_sem.at[at],
                device_id=to,
                device_id_type=MESH,
            ).start()
            return 0

        lax.fori_loop(0, count - 1, send, 0)

        def arrive():
            own.wait()
            part = target.at[pl.ds(0, count - 1)]
            pltpu.make_async_copy(part, part, recv_sem.at[at]).wait()

        def leave():
            part = source.at[pl.ds(0, count - 1)]
            pltpu.make_async_copy(part, part, send_sem.at[at]).wait()

        return arrive, leave

    pl.semaphore_wait(barrier, (GY - 1) + (GX - 1) + 4)
    arrive_one, leave_one = all_to_all(0, GY, send_one, recv_one, gy, on_gy)

    for i in (8, 9):
        loads[i].wait()
    for pair in range(LX // 2):
        rows = mm(t_pair_pool[...], f_rows[pair * PAIR : (pair + 1) * PAIR])
        high, low = halves(rows)
        cells = mm(high, t_lane_pool[...]) + mm(low, t_lane_pool[...])
        pool[pair + 1, 1:3] = cells.astype(BF).reshape(2, 9, 2, HALF)

    def rim(which, dx, dy):
        sx = {-1: pl.ds(1, 1), 0: pl.ds(1, 4), 1: pl.ds(4, 1)}[dx]
        tx = {-1: pl.ds(5, 1), 0: pl.ds(1, 4), 1: pl.ds(0, 1)}[dx]
        sy = {-1: pl.ds(1, 1), 0: pl.ds(1, 2), 1: pl.ds(2, 1)}[dy]
        ty = {-1: pl.ds(3, 1), 0: pl.ds(1, 2), 1: pl.ds(0, 1)}[dy]
        return pltpu.make_async_remote_copy(
            src_ref=pool.at[sx, sy],
            dst_ref=pool.at[tx, ty],
            send_sem=halo_send.at[which],
            recv_sem=halo_recv.at[which],
            device_id=beside(dx, dy),
            device_id_type=MESH,
        )

    rims = [rim(i, dx, dy) for i, (dx, dy) in enumerate(sides)]
    for copy in rims:
        copy.start()

    for i in range(1, 5):
        mine[i].wait()
    for i in range(11, TABLES):
        loads[i].wait()
    wide = mm_nt(t_spread_o[...], pw_in[...]).astype(BF)
    wide = mm_nt(wide, t_spread_o[...]).astype(BF)
    point[...] = wide * t_same[...]
    taps[...] = jnp.zeros_like(taps)
    for c in range(CH):
        taps[c, 0:CH, 0:27] = cw_in[c].astype(FLT)
    flat = taps[...].reshape(24 * CH, 128).astype(BF)
    for at in range(6):
        placed = mm(flat, t_conv_place[at]).astype(BF) * t_conv_same[...]
        conv[at * 24 : (at + 1) * 24] = mm(t_conv_sum[...], placed)

    def widen(at, _):
        w_wide[at, :, 0:MX] = w_in.reshape(3 * CH, CH, 2, MX)[at].astype(FLT).reshape(2 * CH, MX)
        return 0

    lax.fori_loop(0, 3 * CH, widen, 0)
    mixed[...] = jnp.zeros_like(mixed)

    for i in (1, 2):
        loads[i].wait()
    arrive_one()
    lane = lax.broadcasted_iota(jnp.int32, (GX * JS, ROWS), 1)
    part = mm(t_y[...], recv_one[...].reshape(4 * GY, ROWS)).reshape(LY, GX * JS, ROWS)
    chosen = part[0]
    for y in range(1, LY):
        chosen = jnp.where(lax.rem(lane, LY) == y, part[y], chosen)
    high, low = halves(chosen)
    second = mm(high, t_gather[...]) + mm(low, t_gather[...])
    second = [second[:, h * 128 : (h + 1) * 128].reshape(GX, JS, 128) for h in range(2)]
    send_two[...] = jnp.concatenate(second, axis=1).astype(BF)
    arrive_two, leave_two = all_to_all(1, GX, send_two, recv_two, gx, on_gx)

    for i in (10,):
        loads[i].wait()
    for copy in rims:
        copy.wait_recv()

    @pl.when(gx == 0)
    def _():
        pool[0] = jnp.zeros((4, 9, 2, HALF), BF)

    @pl.when(gx == GX - 1)
    def _():
        pool[5] = jnp.zeros((4, 9, 2, HALF), BF)

    @pl.when(gy == 0)
    def _():
        pool[:, 0] = jnp.zeros((6, 9, 2, HALF), BF)

    @pl.when(gy == GY - 1)
    def _():
        pool[:, 3] = jnp.zeros((6, 9, 2, HALF), BF)

    column = jnp.sum(t_spread_o[...].astype(FLT) * bias_in[...], axis=1, keepdims=True)
    spot = lax.broadcasted_iota(jnp.int32, (48, HALF), 1)
    conv_matrix = conv[...].astype(BF)
    for pair in range(LX // 2):
        sums = mm(conv_matrix, pool[pair : pair + 3].reshape(12 * CH, HALF))
        below = jnp.where(spot >= STEPS, pltpu.roll(sums[0:48], STEPS, 1), 0.0)
        above = jnp.where(spot < HALF - STEPS, pltpu.roll(sums[96:144], HALF - STEPS, 1), 0.0)
        high, low = halves(jax.nn.gelu(sums[48:96] + below + above))
        span = slice(pair * PAIR, (pair + 1) * PAIR)
        up = mm(t_row_up[...], mm(high, t_lane_up[...]).astype(BF))
        up = up + mm(t_row_up[...], mm(low, t_lane_up[...]).astype(BF))
        base[span] = mm(point[...], f_rows[span]) + up + column

    for i in (3, 4):
        loads[i].wait()
    arrive_two()
    turned = mm_tn(recv_two[...].reshape(GX * 2 * JS, 128), t_x[...])
    group = lax.broadcasted_iota(jnp.int32, (SLOT, 128), 1) // SLOT
    for at in range(6):
        acc = jnp.zeros((SLOT, 128), FLT)
        for u in range(4):
            piece = turned[u * SLOT : (u + 1) * SLOT, at * 128 : (at + 1) * 128]
            acc = acc + jnp.where(group == u, piece, 0.0)
        acc = acc + pltpu.roll(acc, 64, 1)
        acc = acc + pltpu.roll(acc, 32, 1)
        third[at] = acc

    for j in range(3):
        real = jnp.zeros((CH, 128), FLT)
        imag = jnp.zeros((CH, 128), FLT)
        for c in range(CH):
            w_real = w_wide[j * CH + c, pl.ds(0, CH, stride=2), :]
            w_imag = w_wide[j * CH + c, pl.ds(1, CH, stride=2), :]
            u_real = third[2 * j, c : c + 1, :]
            u_imag = third[2 * j + 1, c : c + 1, :]
            real = real + (w_real * u_real - w_imag * u_imag)
            imag = imag + (w_real * u_imag + w_imag * u_real)
        mixed[2 * j, 0:CH, 0:MX] = real[:, 0:MX]
        mixed[2 * j + 1, 0:CH, 0:MX] = imag[:, 0:MX]

    blocks = []
    for at in range(6):
        value = mixed[at]
        value = value + pltpu.roll(value, 32, 1)
        value = value + pltpu.roll(value, 64, 1)
        tall = [jnp.where(group == u, value, 0.0) for u in range(4)]
        blocks.append(jnp.concatenate(tall, axis=0).astype(BF))
    back = mm_nt(t_ix[...], jnp.concatenate(blocks, axis=1))
    send_three[...] = back.astype(BF).reshape(GX, 2 * JS, 128)
    arrive_three, leave_three = all_to_all(2, GX, send_three, recv_three, gx, on_gx)

    for i in (5, 6, 7):
        loads[i].wait()
    arrive_three()
    wide_in = recv_three[...].astype(FLT)
    sides_in = [wide_in[:, h * JS : (h + 1) * JS].reshape(GX * JS, 128) for h in range(2)]
    spread = mm(jnp.concatenate(sides_in, axis=1).astype(BF), t_spread[...]).astype(BF)
    part = mm(t_iy[...], spread).reshape(LY, 4 * GY, ROWS)
    chosen = part[0]
    for y in range(1, LY):
        chosen = jnp.where(lax.rem(lane, LY) == y, part[y], chosen)
    send_four[...] = chosen.astype(BF).reshape(GY, 4, ROWS)
    arrive_four, leave_four = all_to_all(3, GY, send_four, recv_four, gy, on_gy)

    arrive_four()
    columns = recv_four[...].reshape(4 * GY, ROWS).astype(FLT).T.astype(BF)
    stores = []
    for pair in range(LX // 2):
        span = slice(pair * PAIR, (pair + 1) * PAIR)
        total = mm(columns[span], t_zi[...]) + base[span]
        out_rows[pair * 36 : (pair + 1) * 36] = jax.nn.gelu(total).astype(BF).reshape(36, 4, DEPTH)
        store = pltpu.make_async_copy(
            out_rows.at[pl.ds(pair * 36, 36)],
            out_hbm.at[pl.ds(pair * 36, 36)],
            out_sem.at[pair],
        )
        store.start()
        stores.append(store)
    for leave in (leave_one, leave_two, leave_three, leave_four):
        leave()
    for copy in rims:
        copy.wait_send()
    for store in stores:
        store.wait()


def local(features, mode_weights, point_weight, bias_term, conv_weight):
    tables = make_tables()
    f = features.transpose(0, 2, 1, 3).reshape(LX * CH, LY, DEPTH)
    w = mode_weights.transpose(0, 1, 3, 4, 2, 5)
    taps = conv_weight.transpose(1, 2, 0)
    operands = [f, w, point_weight, bias_term.reshape(1, CH), taps]
    vmem = [
        pltpu.VMEM(f.shape, BF),
        pltpu.VMEM((3,) + w.shape[2:], BF),
        pltpu.VMEM(point_weight.shape, BF),
        pltpu.VMEM((1, CH), FLT),
        pltpu.VMEM(taps.shape, BF),
    ]
    vmem += [pltpu.VMEM(t.shape, BF) for t in tables]
    vmem += [
        pltpu.VMEM((ROWS, DEPTH), BF),
        pltpu.VMEM((GY, 4, ROWS), BF),
        pltpu.VMEM((GY, 4, ROWS), BF),
        pltpu.VMEM((GX, 2 * JS, 128), BF),
        pltpu.VMEM((GX, 2 * JS, 128), BF),
        pltpu.VMEM((GX, 2 * JS, 128), BF),
        pltpu.VMEM((GX, 2 * JS, 128), BF),
        pltpu.VMEM((GY, 4, ROWS), BF),
        pltpu.VMEM((GY, 4, ROWS), BF),
        pltpu.VMEM((6, 4, 9, 2, HALF), BF),
        pltpu.VMEM((PAIR, PAIR), BF),
        pltpu.VMEM((CH, 24, 128), FLT),
        pltpu.VMEM((144, 12 * CH), FLT),
        pltpu.VMEM((3 * CH, 2 * CH, 128), FLT),
        pltpu.VMEM((6, SLOT, 128), FLT),
        pltpu.VMEM((6, SLOT, 128), FLT),
        pltpu.VMEM((ROWS, DEPTH), FLT),
        pltpu.VMEM(f.shape, BF),
        pltpu.SemaphoreType.DMA((5,)),
        pltpu.SemaphoreType.DMA((TABLES,)),
        pltpu.SemaphoreType.DMA((4,)),
        pltpu.SemaphoreType.DMA((4,)),
        pltpu.SemaphoreType.DMA((4,)),
        pltpu.SemaphoreType.DMA((8,)),
        pltpu.SemaphoreType.DMA((8,)),
        pltpu.SemaphoreType.DMA((4,)),
    ]
    out = pl.pallas_call(
        kernel,
        out_shape=jax.ShapeDtypeStruct(f.shape, BF),
        in_specs=[pl.BlockSpec(memory_space=pltpu.HBM)] * (5 + len(tables)),
        out_specs=pl.BlockSpec(memory_space=pl.ANY),
        scratch_shapes=vmem,
        compiler_params=pltpu.CompilerParams(
            collective_id=0, has_side_effects=True, vmem_limit_bytes=48 << 20
        ),
        name="layer",
    )(*[pltpu.with_memory_space_constraint(t, pltpu.HBM) for t in operands + [jnp.asarray(t) for t in tables]])
    return out.reshape(LX, CH, LY, DEPTH).transpose(0, 2, 1, 3)


def solution(mesh):
    in_specs = (P("gx", "gy", None, None), P("gy", None, None, None, None, None), P(), P(), P())
    out_specs = P("gx", "gy", None, None)
    return jax.shard_map(local, mesh=mesh, in_specs=in_specs, out_specs=out_specs, check_vma=False)
```

```python
import math

import jax
import jax.numpy as jnp
import ml_dtypes
import numpy as np
from jax import lax
from jax.experimental import pallas as pl
from jax.experimental.pallas import tpu as pltpu
from jax.sharding import PartitionSpec as P

BF = jnp.bfloat16
FLT = jnp.float32
MESH = pl.DeviceIdType.MESH

GRID_Z, STEPS, CH = 64, 8, 18
MX, MY, MZ, MT = 24, 24, 16, 4
GX, GY = 16, 32
LX, LY = 8, 4
ROWS = LX * CH * LY
PAIR = 2 * CH * LY
DEPTH = GRID_Z * STEPS
HALF = DEPTH // 2
MODES = MZ * MT
JS = 8
SLOT = 32
TABLES = 17


def frequencies(number):
    places = np.arange(number, dtype=np.int32)
    return np.where(places < number // 2, places, places - number)


def angles_of(number, length):
    places = np.arange(length, dtype=np.int32)
    fraction = np.mod(frequencies(number)[:, None] * places[None, :], length).astype(np.float32)
    return np.float32(2.0 * math.pi) * (fraction / np.float32(length))


def rounded(table):
    return np.asarray(table, np.float32).astype(ml_dtypes.bfloat16).astype(np.float32)


def forward_table(number, length):
    angles = angles_of(number, length).T
    cosine = np.cos(angles) / np.float32(math.sqrt(length))
    sine = np.sin(angles) / np.float32(math.sqrt(length))
    return rounded(np.stack([np.stack([cosine, -sine], 1), np.stack([sine, cosine], 1)], 0))


def inverse_table(number, length):
    angles = angles_of(number, length)
    cosine = np.cos(angles) / np.float32(math.sqrt(number))
    sine = np.sin(angles) / np.float32(math.sqrt(number))
    return rounded(np.stack([np.stack([cosine, sine], 1), np.stack([-sine, cosine], 1)], 0))


def depth_tables():
    along_z = angles_of(MZ, GRID_Z)
    time_freq = np.arange(MT, dtype=np.int32)
    time_pos = np.arange(STEPS, dtype=np.int32)
    along_t = np.mod(time_freq[:, None] * time_pos[None, :], STEPS).astype(np.float32)
    along_t = np.float32(2.0 * math.pi) * along_t / np.float32(STEPS)
    angles = along_z[:, None, :, None] + along_t[None, :, None, :]
    cosine, sine = np.cos(angles), np.sin(angles)
    forward = np.stack([cosine, -sine], 2) / np.float32(math.sqrt(DEPTH))
    forward = forward.reshape(2 * MODES, DEPTH)
    factor = np.where(time_freq == 0, 1.0, 2.0).astype(np.float32)[None, :, None, None]
    factor = factor / np.float32(math.sqrt(MODES))
    inverse = np.stack([factor * cosine, -factor * sine], 2).reshape(2 * MODES, DEPTH)
    return rounded(forward), rounded(inverse)


def make_tables():
    zt_forward, zt_inverse = depth_tables()
    yf, yi = forward_table(MY, GY * LY), inverse_table(MY, GY * LY)
    xf, xi = forward_table(MX, GX * LX), inverse_table(MX, GX * LX)
    per = MY // 8
    block = yf.reshape(2, GY, LY, 2, 8, per)
    ty = np.zeros((LY, 8, JS, GY, 2), np.float32)
    ty[:, :, : 2 * per] = np.einsum("rgysaj->yajsgr", block).reshape(LY, 8, 2 * per, GY, 2)
    ty = ty.reshape(LY * 8 * JS, GY * 2)
    eyex, eyec, eyey = np.eye(LX), np.eye(CH, SLOT), np.eye(LY)
    gather = np.einsum("xX,cC,y->xcyXC", eyex, eyec, np.ones(LY)).reshape(ROWS, LX * SLOT)
    block = xf.reshape(2, GX, 2, 4, 2, MX)
    eyej = np.eye(per)
    tx = np.zeros((GX, 2, JS, per, 2, 4, SLOT), np.float32)
    tx[:, :, : 2 * per, :, :, :, :MX] = np.einsum("rahusk,ij->ahirjsuk", block, eyej).reshape(
        GX, 2, 2 * per, per, 2, 4, MX
    )
    tx = tx.reshape(GX * 2 * JS, per * 2 * 4 * SLOT)
    block = xi.reshape(2, MX, 2, GX, 2, 4)
    tix = np.zeros((GX, 2, JS, per, 2, 4, SLOT), np.float32)
    tix[:, :, : 2 * per, :, :, :, :MX] = np.einsum("rksahu,ij->ahisjruk", block, eyej).reshape(
        GX, 2, 2 * per, per, 2, 4, MX
    )
    tix = tix.reshape(GX * 2 * JS, per * 2 * 4 * SLOT)
    block = yi.reshape(2, 8, per, 2, GY, LY)
    tiy = np.zeros((LY, GY, 2, 8, JS), np.float32)
    tiy[..., : 2 * per] = np.einsum("rajsgy->ygsajr", block).reshape(LY, GY, 2, 8, 2 * per)
    tiy = tiy.reshape(LY * GY * 2, 8 * JS)
    zt_forward = zt_forward.reshape(GY, 2, 2, DEPTH).transpose(1, 0, 2, 3).reshape(2 * MODES, DEPTH)
    zt_inverse = zt_inverse.reshape(GY, 2, 2, DEPTH).transpose(1, 0, 2, 3).reshape(2, MODES, DEPTH)
    pair_pool = np.einsum("x,cC,yY->YCxcy", np.ones(2), np.eye(CH), np.repeat(np.eye(2), 2, 0))
    pair_pool = pair_pool.reshape(2 * CH, PAIR)
    lane_up = np.einsum("zZ,tT->ZTzt", np.repeat(np.eye(GRID_Z // 2), 2, 0), np.eye(STEPS))
    lane_up = lane_up.reshape(HALF, DEPTH)
    lane_pool = 0.125 * lane_up.T
    row_up = np.zeros((PAIR, 2, 24), np.float32)
    row_up[:, :, :CH] = pair_pool.T.reshape(PAIR, 2, CH)
    row_up = row_up.reshape(PAIR, 48)
    spread_o = np.einsum("x,oO,y->xoyO", np.ones(2), np.eye(CH), np.ones(LY)).reshape(PAIR, CH)
    same = np.einsum("xX,oc,yY->xoyXcY", np.eye(2), np.ones((CH, CH)), eyey).reshape(PAIR, PAIR)
    eyecc = np.eye(CH, dtype=np.float32)
    conv_place = np.zeros((3, 2, 128, 3, 4, CH), np.float32)
    for dx in range(3):
        for dy in range(3):
            for dz in range(3):
                for at in range(2):
                    conv_place[dz, at, 9 * dx + 3 * dy + dz, dx, dy + at] = 1.0
    conv_place = conv_place.reshape(6, 128, 12 * CH)
    conv_same = np.einsum("cC,o,d->coCd", eyecc, np.ones(24), np.ones(12))
    conv_same = conv_same.transpose(0, 1, 3, 2).reshape(24 * CH, 12 * CH)
    conv_sum = np.einsum("c,oO->ocO", np.ones(CH), np.eye(24)).reshape(24, 24 * CH)
    return [
        np.asarray(t, np.float32).astype(ml_dtypes.bfloat16)
        for t in (
            zt_forward,
            ty,
            gather,
            tx,
            tix,
            gather.T,
            tiy,
            zt_inverse,
            pair_pool,
            lane_pool,
            lane_up,
            row_up,
            spread_o,
            same,
            conv_place,
            conv_same,
            conv_sum,
        )
    ]


def mm(a, b):
    return jnp.dot(a, b, preferred_element_type=FLT)


def mm_nt(a, b):
    return lax.dot_general(a, b, (((1,), (1,)), ((), ())), preferred_element_type=FLT)


def mm_tn(a, b):
    return lax.dot_general(a, b, (((0,), (0,)), ((), ())), preferred_element_type=FLT)


def halves(value):
    high = value.astype(BF)
    return high, (value - high.astype(FLT)).astype(BF)


def kernel(*refs):
    (f_hbm, w_hbm, pw_hbm, bias_hbm, cw_hbm), refs = refs[:5], refs[5:]
    tables_hbm, refs = refs[:TABLES], refs[TABLES:]
    out_hbm, refs = refs[0], refs[1:]
    (f_in, w_in, pw_in, bias_in, cw_in), refs = refs[:5], refs[5:]
    tables, refs = refs[:TABLES], refs[TABLES:]
    (
        f_rows,
        send_one,
        recv_one,
        send_two,
        recv_two,
        send_three,
        recv_three,
        send_four,
        recv_four,
        pool,
        point,
        taps,
        conv,
        w_wide,
        third,
        mixed,
        base,
        out_rows,
        in_sem,
        table_sem,
        send_sem,
        recv_sem,
        halo_send,
        halo_recv,
        out_sem,
    ) = refs
    (
        t_zf,
        t_y,
        t_gather,
        t_x,
        t_ix,
        t_spread,
        t_iy,
        t_zi,
        t_pair_pool,
        t_lane_pool,
        t_lane_up,
        t_row_up,
        t_spread_o,
        t_same,
        t_conv_place,
        t_conv_same,
        t_conv_sum,
    ) = tables
    gx = lax.axis_index("gx")
    gy = lax.axis_index("gy")
    barrier = pltpu.get_barrier_semaphore()

    def far_first(step, count):
        sign = 1 - 2 * lax.rem(step, 2)
        return count // 2 + sign * lax.div(step + 1, 2)

    far = (2, 1, 3, 0)
    inner = lax.rem(gy, 4)
    lows = [lax.rem(inner + k, 4) for k in far]
    xs = [4 * lax.rem(lax.div(gx, 4) + k, 4) for k in far]

    def each_gy(act):
        def ring(step, _):
            plane = 4 * lax.rem(lax.div(gy, 4) + far_first(step, 8), 8)
            for k in range(4):
                act(plane + lows[k])
            return 0

        lax.fori_loop(0, 7, ring, 0)
        for k in range(3):
            act(gy - inner + lows[k])

    def each_gx(act):
        for k in far:
            y = lax.rem(lax.rem(gx, 4) + k, 4)
            for i in range(4 if k else 3):
                act(xs[i] + y)

    def greet(target):
        pl.semaphore_signal(barrier, inc=1, device_id=target, device_id_type=MESH)

    mine = [
        pltpu.make_async_copy(f_hbm, f_in, in_sem.at[0]),
        pltpu.make_async_copy(
            w_hbm.at[gx // 8, pl.ds(3 * lax.rem(gx, 8), 3)], w_in, in_sem.at[1]
        ),
        pltpu.make_async_copy(pw_hbm, pw_in, in_sem.at[2]),
        pltpu.make_async_copy(bias_hbm, bias_in, in_sem.at[3]),
        pltpu.make_async_copy(cw_hbm, cw_in, in_sem.at[4]),
    ]
    loads = [
        pltpu.make_async_copy(tables_hbm[i], tables[i], table_sem.at[i]) for i in range(TABLES)
    ]
    loads[0].start()
    mine[0].start()

    each_gx(lambda to: greet((to, gy)))
    each_gy(lambda to: greet((gx, to)))
    sides = [(dx, dy) for dx in (-1, 0, 1) for dy in (-1, 0, 1) if (dx, dy) != (0, 0)]

    def beside(dx, dy):
        return (lax.rem(gx + dx + GX, GX), lax.rem(gy + dy + GY, GY))

    for dx, dy in sides:
        if dx != 0 and dy != 0:
            greet(beside(dx, dy))
    for load in loads[1:]:
        load.start()
    for load in mine[1:]:
        load.start()

    mine[0].wait()
    loads[0].wait()
    f_rows[...] = f_in.reshape(ROWS, DEPTH)[...]
    hat = mm_nt(t_zf[...], f_rows[...]).astype(BF)
    for m in range(2):
        send_one[m] = hat[m * MODES : (m + 1) * MODES].reshape(GY, 2, ROWS)

    def along_gy(at, source, target):
        own = pltpu.make_async_copy(source.at[gy], target.at[gy], recv_sem.at[at])
        own.start()

        def send(to):
            pltpu.make_async_remote_copy(
                src_ref=source.at[to],
                dst_ref=target.at[gy],
                send_sem=send_sem.at[at],
                recv_sem=recv_sem.at[at],
                device_id=(gx, to),
                device_id_type=MESH,
            ).start()

        each_gy(send)

    def arrived(at, whole):
        pltpu.make_async_copy(whole, whole, recv_sem.at[at]).wait()

    def left(at, source, count):
        part = source.at[pl.ds(0, count)]
        pltpu.make_async_copy(part, part, send_sem.at[at]).wait()

    pl.semaphore_wait(barrier, (GY - 1) + (GX - 1) + 4)
    for m in range(2):
        along_gy(m, send_one.at[m], recv_one.at[m])

    for i in (8, 9):
        loads[i].wait()
    for pair in range(LX // 2):
        rows = mm(t_pair_pool[...], f_rows[pair * PAIR : (pair + 1) * PAIR])
        high, low = halves(rows)
        cells = mm(high, t_lane_pool[...]) + mm(low, t_lane_pool[...])
        pool[pair + 1, 1:3] = cells.astype(BF).reshape(2, 9, 2, HALF)

    def rim(which, dx, dy):
        sx = {-1: pl.ds(1, 1), 0: pl.ds(1, 4), 1: pl.ds(4, 1)}[dx]
        tx = {-1: pl.ds(5, 1), 0: pl.ds(1, 4), 1: pl.ds(0, 1)}[dx]
        sy = {-1: pl.ds(1, 1), 0: pl.ds(1, 2), 1: pl.ds(2, 1)}[dy]
        ty = {-1: pl.ds(3, 1), 0: pl.ds(1, 2), 1: pl.ds(0, 1)}[dy]
        return pltpu.make_async_remote_copy(
            src_ref=pool.at[sx, sy],
            dst_ref=pool.at[tx, ty],
            send_sem=halo_send.at[which],
            recv_sem=halo_recv.at[which],
            device_id=beside(dx, dy),
            device_id_type=MESH,
        )

    rims = [rim(i, dx, dy) for i, (dx, dy) in enumerate(sides)]
    for copy in rims:
        copy.start()

    mine[1].wait()

    def widen(at, _):
        w_wide[at, :, 0:MX] = w_in.reshape(3 * CH, CH, 2, MX)[at].astype(FLT).reshape(2 * CH, MX)
        return 0

    lax.fori_loop(0, 3 * CH, widen, 0)
    mixed[...] = jnp.zeros_like(mixed)

    for i in (1, 2):
        loads[i].wait()
    lane = lax.rem(lax.broadcasted_iota(jnp.int32, (8 * JS, ROWS), 1), LY)
    for m in range(2):
        arrived(m, recv_one.at[m])
        part = mm(t_y[...], recv_one[m].reshape(2 * GY, ROWS)).reshape(LY, 8 * JS, ROWS)
        chosen = part[0]
        for y in range(1, LY):
            chosen = jnp.where(lane == y, part[y], chosen)
        both = mm(jnp.concatenate(halves(chosen), axis=0), t_gather[...])
        second = both[: 8 * JS] + both[8 * JS :]
        second = [second[:, h * 128 : (h + 1) * 128].reshape(8, JS, 128) for h in range(2)]
        send_two[8 * m : 8 * m + 8] = jnp.concatenate(second, axis=1).astype(BF)

        def send(step, _):
            x = 2 * m + lax.rem(step, 2)
            y = lax.rem(lax.rem(gx, 4) + far_first(lax.div(step, 2), 4), 4)
            to = 4 * x + y

            @pl.when(to != gx)
            def _():
                pltpu.make_async_remote_copy(
                    src_ref=send_two.at[to],
                    dst_ref=recv_two.at[gx],
                    send_sem=send_sem.at[2],
                    recv_sem=recv_sem.at[2],
                    device_id=(to, gy),
                    device_id_type=MESH,
                ).start()

            return 0

        lax.fori_loop(0, 8, send, 0)
    pltpu.make_async_copy(send_two.at[gx], recv_two.at[gx], recv_sem.at[2]).start()

    for i in (3, 4):
        loads[i].wait()
    arrived(2, recv_two)
    turned = mm_tn(recv_two[...].reshape(GX * 2 * JS, 128), t_x[...])
    group = lax.broadcasted_iota(jnp.int32, (SLOT, 128), 1) // SLOT
    for at in range(6):
        acc = jnp.zeros((SLOT, 128), FLT)
        for u in range(4):
            piece = turned[u * SLOT : (u + 1) * SLOT, at * 128 : (at + 1) * 128]
            acc = acc + jnp.where(group == u, piece, 0.0)
        acc = acc + pltpu.roll(acc, 64, 1)
        acc = acc + pltpu.roll(acc, 32, 1)
        third[at] = acc

    for j in range(3):
        real = jnp.zeros((CH, 128), FLT)
        imag = jnp.zeros((CH, 128), FLT)
        for c in range(CH):
            w_real = w_wide[j * CH + c, pl.ds(0, CH, stride=2), :]
            w_imag = w_wide[j * CH + c, pl.ds(1, CH, stride=2), :]
            u_real = third[2 * j, c : c + 1, :]
            u_imag = third[2 * j + 1, c : c + 1, :]
            real = real + (w_real * u_real - w_imag * u_imag)
            imag = imag + (w_real * u_imag + w_imag * u_real)
        mixed[2 * j, 0:CH, 0:MX] = real[:, 0:MX]
        mixed[2 * j + 1, 0:CH, 0:MX] = imag[:, 0:MX]

    blocks = []
    for at in range(6):
        value = mixed[at]
        value = value + pltpu.roll(value, 32, 1)
        value = value + pltpu.roll(value, 64, 1)
        tall = [jnp.where(group == u, value, 0.0) for u in range(4)]
        blocks.append(jnp.concatenate(tall, axis=0).astype(BF))
    back = mm_nt(t_ix[...], jnp.concatenate(blocks, axis=1))
    send_three[...] = back.astype(BF).reshape(GX, 2 * JS, 128)
    at_three = 3 + lax.div(gx, 8)
    pltpu.make_async_copy(send_three.at[gx], recv_three.at[gx], recv_sem.at[at_three]).start()

    def send(to):
        pltpu.make_async_remote_copy(
            src_ref=send_three.at[to],
            dst_ref=recv_three.at[gx],
            send_sem=send_sem.at[3],
            recv_sem=recv_sem.at[at_three],
            device_id=(to, gy),
            device_id_type=MESH,
        ).start()

    each_gx(send)

    for i in (2, 3, 4):
        mine[i].wait()
    for i in range(10, TABLES):
        loads[i].wait()
    wide = mm_nt(t_spread_o[...], pw_in[...]).astype(BF)
    wide = mm_nt(wide, t_spread_o[...]).astype(BF)
    point[...] = wide * t_same[...]
    taps[...] = jnp.zeros_like(taps)
    for c in range(CH):
        taps[c, 0:CH, 0:27] = cw_in[c].astype(FLT)
    flat = taps[...].reshape(24 * CH, 128).astype(BF)
    for at in range(6):
        placed = mm(flat, t_conv_place[at]).astype(BF) * t_conv_same[...]
        conv[at * 24 : (at + 1) * 24] = mm(t_conv_sum[...], placed)

    for copy in rims:
        copy.wait_recv()

    @pl.when(gx == 0)
    def _():
        pool[0] = jnp.zeros((4, 9, 2, HALF), BF)

    @pl.when(gx == GX - 1)
    def _():
        pool[5] = jnp.zeros((4, 9, 2, HALF), BF)

    @pl.when(gy == 0)
    def _():
        pool[:, 0] = jnp.zeros((6, 9, 2, HALF), BF)

    @pl.when(gy == GY - 1)
    def _():
        pool[:, 3] = jnp.zeros((6, 9, 2, HALF), BF)

    for i in (5, 6, 7):
        loads[i].wait()
    for m in range(2):
        mine_three = recv_three.at[pl.ds(8 * m, 8)]
        arrived(3 + m, mine_three)
        wide_in = mine_three[...].astype(FLT)
        sides_in = [wide_in[:, h * JS : (h + 1) * JS].reshape(8 * JS, 128) for h in range(2)]
        spread = mm(jnp.concatenate(sides_in, axis=1).astype(BF), t_spread[...]).astype(BF)
        part = mm(t_iy[...], spread).reshape(LY, 2 * GY, ROWS)
        chosen = part[0]
        for y in range(1, LY):
            chosen = jnp.where(lane == y, part[y], chosen)
        send_four[m] = chosen.astype(BF).reshape(GY, 2, ROWS)
        along_gy(5 + m, send_four.at[m], recv_four.at[m])

    column = jnp.sum(t_spread_o[...].astype(FLT) * bias_in[...], axis=1, keepdims=True)
    spot = lax.broadcasted_iota(jnp.int32, (48, HALF), 1)
    conv_matrix = conv[...].astype(BF)
    for pair in range(LX // 2):
        sums = mm(conv_matrix, pool[pair : pair + 3].reshape(12 * CH, HALF))
        below = jnp.where(spot >= STEPS, pltpu.roll(sums[0:48], STEPS, 1), 0.0)
        above = jnp.where(spot < HALF - STEPS, pltpu.roll(sums[96:144], HALF - STEPS, 1), 0.0)
        high, low = halves(jax.nn.gelu(sums[48:96] + below + above))
        span = slice(pair * PAIR, (pair + 1) * PAIR)
        up = mm(t_row_up[...], mm(high, t_lane_up[...]).astype(BF))
        up = up + mm(t_row_up[...], mm(low, t_lane_up[...]).astype(BF))
        base[span] = mm(point[...], f_rows[span]) + up + column

    arrived(5, recv_four.at[0])
    columns = recv_four[0].reshape(2 * GY, ROWS).astype(FLT).T.astype(BF)
    for pair in range(LX // 2):
        span = slice(pair * PAIR, (pair + 1) * PAIR)
        base[span] += mm(columns[span], t_zi[0])
    arrived(6, recv_four.at[1])
    columns = recv_four[1].reshape(2 * GY, ROWS).astype(FLT).T.astype(BF)
    for pair in range(LX // 2):
        span = slice(pair * PAIR, (pair + 1) * PAIR)
        total = mm(columns[span], t_zi[1]) + base[span]
        out_hbm[pair * 36 : (pair + 1) * 36] = jax.nn.gelu(total).astype(BF).reshape(36, 4, DEPTH)
    for m in range(2):
        left(m, send_one.at[m], GY - 1)
        left(5 + m, send_four.at[m], GY - 1)
    left(2, send_two, GX - 1)
    left(3, send_three, GX - 1)
    for copy in rims:
        copy.wait_send()


def local(features, mode_weights, point_weight, bias_term, conv_weight):
    tables = make_tables()
    f = features.transpose(0, 2, 1, 3).reshape(LX * CH, LY, DEPTH)
    w = mode_weights.transpose(0, 1, 3, 4, 2, 5)
    taps = conv_weight.transpose(1, 2, 0)
    operands = [f, w, point_weight, bias_term.reshape(1, CH), taps]
    vmem = [
        pltpu.VMEM(f.shape, BF),
        pltpu.VMEM((3,) + w.shape[2:], BF),
        pltpu.VMEM(point_weight.shape, BF),
        pltpu.VMEM((1, CH), FLT),
        pltpu.VMEM(taps.shape, BF),
    ]
    vmem += [pltpu.VMEM(t.shape, BF) for t in tables]
    vmem += [
        pltpu.VMEM((ROWS, DEPTH), BF),
        pltpu.VMEM((2, GY, 2, ROWS), BF),
        pltpu.VMEM((2, GY, 2, ROWS), BF),
        pltpu.VMEM((GX, 2 * JS, 128), BF),
        pltpu.VMEM((GX, 2 * JS, 128), BF),
        pltpu.VMEM((GX, 2 * JS, 128), BF),
        pltpu.VMEM((GX, 2 * JS, 128), BF),
        pltpu.VMEM((2, GY, 2, ROWS), BF),
        pltpu.VMEM((2, GY, 2, ROWS), BF),
        pltpu.VMEM((6, 4, 9, 2, HALF), BF),
        pltpu.VMEM((PAIR, PAIR), BF),
        pltpu.VMEM((CH, 24, 128), FLT),
        pltpu.VMEM((144, 12 * CH), FLT),
        pltpu.VMEM((3 * CH, 2 * CH, 128), FLT),
        pltpu.VMEM((6, SLOT, 128), FLT),
        pltpu.VMEM((6, SLOT, 128), FLT),
        pltpu.VMEM((ROWS, DEPTH), FLT),
        pltpu.VMEM(f.shape, BF),
        pltpu.SemaphoreType.DMA((5,)),
        pltpu.SemaphoreType.DMA((TABLES,)),
        pltpu.SemaphoreType.DMA((7,)),
        pltpu.SemaphoreType.DMA((7,)),
        pltpu.SemaphoreType.DMA((8,)),
        pltpu.SemaphoreType.DMA((8,)),
        pltpu.SemaphoreType.DMA((4,)),
    ]
    out = pl.pallas_call(
        kernel,
        out_shape=jax.ShapeDtypeStruct(f.shape, BF),
        in_specs=[pl.BlockSpec(memory_space=pltpu.HBM)] * (5 + len(tables)),
        out_specs=pl.BlockSpec(memory_space=pltpu.VMEM),
        scratch_shapes=vmem,
        compiler_params=pltpu.CompilerParams(
            collective_id=0, has_side_effects=True, vmem_limit_bytes=48 << 20
        ),
        name="layer",
    )(*[pltpu.with_memory_space_constraint(t, pltpu.HBM) for t in operands + [jnp.asarray(t) for t in tables]])
    return out.reshape(LX, CH, LY, DEPTH).transpose(0, 2, 1, 3)


def solution(mesh):
    in_specs = (P("gx", "gy", None, None), P("gy", None, None, None, None, None), P(), P(), P())
    out_specs = P("gx", "gy", None, None)
    return jax.shard_map(local, mesh=mesh, in_specs=in_specs, out_specs=out_specs, check_vma=False)
```

```python
import math

import jax
import jax.numpy as jnp
import ml_dtypes
import numpy as np
from jax import lax
from jax.experimental import pallas as pl
from jax.experimental.pallas import tpu as pltpu
from jax.sharding import PartitionSpec as P

BF = jnp.bfloat16
FLT = jnp.float32
MESH = pl.DeviceIdType.MESH

GRID_Z, STEPS, CH = 64, 8, 18
MX, MY, MZ, MT = 24, 24, 16, 4
GX, GY = 16, 32
LX, LY = 8, 4
ROWS = LX * CH * LY
PAIR = 2 * CH * LY
DEPTH = GRID_Z * STEPS
HALF = DEPTH // 2
MODES = MZ * MT
JS = 8
SLOT = 32
TABLES = 17


def frequencies(number):
    places = np.arange(number, dtype=np.int32)
    return np.where(places < number // 2, places, places - number)


def angles_of(number, length):
    places = np.arange(length, dtype=np.int32)
    fraction = np.mod(frequencies(number)[:, None] * places[None, :], length).astype(np.float32)
    return np.float32(2.0 * math.pi) * (fraction / np.float32(length))


def rounded(table):
    return np.asarray(table, np.float32).astype(ml_dtypes.bfloat16).astype(np.float32)


def forward_table(number, length):
    angles = angles_of(number, length).T
    cosine = np.cos(angles) / np.float32(math.sqrt(length))
    sine = np.sin(angles) / np.float32(math.sqrt(length))
    return rounded(np.stack([np.stack([cosine, -sine], 1), np.stack([sine, cosine], 1)], 0))


def inverse_table(number, length):
    angles = angles_of(number, length)
    cosine = np.cos(angles) / np.float32(math.sqrt(number))
    sine = np.sin(angles) / np.float32(math.sqrt(number))
    return rounded(np.stack([np.stack([cosine, sine], 1), np.stack([-sine, cosine], 1)], 0))


def depth_tables():
    along_z = angles_of(MZ, GRID_Z)
    time_freq = np.arange(MT, dtype=np.int32)
    time_pos = np.arange(STEPS, dtype=np.int32)
    along_t = np.mod(time_freq[:, None] * time_pos[None, :], STEPS).astype(np.float32)
    along_t = np.float32(2.0 * math.pi) * along_t / np.float32(STEPS)
    angles = along_z[:, None, :, None] + along_t[None, :, None, :]
    cosine, sine = np.cos(angles), np.sin(angles)
    forward = np.stack([cosine, -sine], 2) / np.float32(math.sqrt(DEPTH))
    forward = forward.reshape(2 * MODES, DEPTH)
    factor = np.where(time_freq == 0, 1.0, 2.0).astype(np.float32)[None, :, None, None]
    factor = factor / np.float32(math.sqrt(MODES))
    inverse = np.stack([factor * cosine, -factor * sine], 2).reshape(2 * MODES, DEPTH)
    return rounded(forward), rounded(inverse)


def make_tables():
    zt_forward, zt_inverse = depth_tables()
    yf, yi = forward_table(MY, GY * LY), inverse_table(MY, GY * LY)
    xf, xi = forward_table(MX, GX * LX), inverse_table(MX, GX * LX)
    per = MY // 8
    block = yf.reshape(2, GY, LY, 2, 8, per)
    ty = np.zeros((LY, 8, JS, GY, 2), np.float32)
    ty[:, :, : 2 * per] = np.einsum("rgysaj->yajsgr", block).reshape(LY, 8, 2 * per, GY, 2)
    ty = ty.reshape(LY * 8 * JS, GY * 2)
    eyex, eyec, eyey = np.eye(LX), np.eye(CH, SLOT), np.eye(LY)
    gather = np.einsum("xX,cC,y->xcyXC", eyex, eyec, np.ones(LY)).reshape(ROWS, LX * SLOT)
    block = xf.reshape(2, GX, 2, 4, 2, MX)
    eyej = np.eye(per)
    tx = np.zeros((GX, 2, JS, per, 2, 4, SLOT), np.float32)
    tx[:, :, : 2 * per, :, :, :, :MX] = np.einsum("rahusk,ij->ahirjsuk", block, eyej).reshape(
        GX, 2, 2 * per, per, 2, 4, MX
    )
    tx = tx.reshape(GX * 2 * JS, per * 2 * 4 * SLOT)
    block = xi.reshape(2, MX, 2, GX, 2, 4)
    tix = np.zeros((GX, 2, JS, per, 2, 4, SLOT), np.float32)
    tix[:, :, : 2 * per, :, :, :, :MX] = np.einsum("rksahu,ij->ahisjruk", block, eyej).reshape(
        GX, 2, 2 * per, per, 2, 4, MX
    )
    tix = tix.reshape(GX * 2 * JS, per * 2 * 4 * SLOT)
    block = yi.reshape(2, 8, per, 2, GY, LY)
    tiy = np.zeros((LY, GY, 2, 8, JS), np.float32)
    tiy[..., : 2 * per] = np.einsum("rajsgy->ygsajr", block).reshape(LY, GY, 2, 8, 2 * per)
    tiy = tiy.reshape(LY * GY * 2, 8 * JS)
    zt_forward = zt_forward.reshape(GY, 2, 2, DEPTH).transpose(1, 0, 2, 3).reshape(2 * MODES, DEPTH)
    zt_inverse = zt_inverse.reshape(GY, 2, 2, DEPTH).transpose(1, 0, 2, 3).reshape(2, MODES, DEPTH)
    pair_pool = np.einsum("x,cC,yY->YCxcy", np.ones(2), np.eye(CH), np.repeat(np.eye(2), 2, 0))
    pair_pool = pair_pool.reshape(2 * CH, PAIR)
    lane_up = np.einsum("zZ,tT->ZTzt", np.repeat(np.eye(GRID_Z // 2), 2, 0), np.eye(STEPS))
    lane_up = lane_up.reshape(HALF, DEPTH)
    lane_pool = 0.125 * lane_up.T
    row_up = np.zeros((PAIR, 2, 24), np.float32)
    row_up[:, :, :CH] = pair_pool.T.reshape(PAIR, 2, CH)
    row_up = row_up.reshape(PAIR, 48)
    spread_o = np.einsum("x,oO,y->xoyO", np.ones(2), np.eye(CH), np.ones(LY)).reshape(PAIR, CH)
    same = np.einsum("xX,oc,yY->xoyXcY", np.eye(2), np.ones((CH, CH)), eyey).reshape(PAIR, PAIR)
    eyecc = np.eye(CH, dtype=np.float32)
    conv_place = np.zeros((3, 2, 128, 3, 4, CH), np.float32)
    for dx in range(3):
        for dy in range(3):
            for dz in range(3):
                for at in range(2):
                    conv_place[dz, at, 9 * dx + 3 * dy + dz, dx, dy + at] = 1.0
    conv_place = conv_place.reshape(6, 128, 12 * CH)
    conv_same = np.einsum("cC,o,d->coCd", eyecc, np.ones(24), np.ones(12))
    conv_same = conv_same.transpose(0, 1, 3, 2).reshape(24 * CH, 12 * CH)
    conv_sum = np.einsum("c,oO->ocO", np.ones(CH), np.eye(24)).reshape(24, 24 * CH)
    return [
        np.asarray(t, np.float32).astype(ml_dtypes.bfloat16)
        for t in (
            zt_forward,
            ty,
            gather,
            tx,
            tix,
            gather.T,
            tiy,
            zt_inverse,
            pair_pool,
            lane_pool,
            lane_up,
            row_up,
            spread_o,
            same,
            conv_place,
            conv_same,
            conv_sum,
        )
    ]


def mm(a, b):
    return jnp.dot(a, b, preferred_element_type=FLT)


def mm_nt(a, b):
    return lax.dot_general(a, b, (((1,), (1,)), ((), ())), preferred_element_type=FLT)


def mm_tn(a, b):
    return lax.dot_general(a, b, (((0,), (0,)), ((), ())), preferred_element_type=FLT)


def halves(value):
    high = value.astype(BF)
    return high, (value - high.astype(FLT)).astype(BF)


def kernel(*refs):
    (f_hbm, w_hbm, pw_hbm, bias_hbm, cw_hbm), refs = refs[:5], refs[5:]
    tables_hbm, refs = refs[:TABLES], refs[TABLES:]
    out_ref, refs = refs[0], refs[1:]
    (f_in, w_in, pw_in, bias_in, cw_in), refs = refs[:5], refs[5:]
    tables, refs = refs[:TABLES], refs[TABLES:]
    (
        f_rows,
        send_one,
        recv_one,
        send_two,
        recv_two,
        send_three,
        recv_three,
        send_four,
        recv_four,
        pool,
        point,
        taps,
        conv,
        w_wide,
        third,
        base,
        in_sem,
        table_sem,
        send_sem,
        recv_sem,
        halo_send,
        halo_recv,
        heard,
    ) = refs
    (
        t_zf,
        t_y,
        t_gather,
        t_x,
        t_ix,
        t_spread,
        t_iy,
        t_zi,
        t_pair_pool,
        t_lane_pool,
        t_lane_up,
        t_row_up,
        t_spread_o,
        t_same,
        t_conv_place,
        t_conv_same,
        t_conv_sum,
    ) = tables
    gx = lax.axis_index("gx")
    gy = lax.axis_index("gy")
    barrier = pltpu.get_barrier_semaphore()

    far = (2, 1, 3, 0)
    inner = lax.rem(gy, 4)
    lows = [lax.rem(inner + k, 4) for k in far]
    xs = [4 * lax.rem(lax.div(gx, 4) + k, 4) for k in far]

    planes = [4 * lax.rem(lax.div(gy, 4) + k, 8) for k in range(1, 8)]

    def each_gy(act):
        for step in (4, 3, 5, 2, 6, 1, 7):
            plane = planes[step - 1]
            for k in range(4):
                act(plane + lows[k])
        for k in range(3):
            act(gy - inner + lows[k])

    def each_gx(act):
        for k in far:
            y = lax.rem(lax.rem(gx, 4) + k, 4)
            for i in range(4 if k else 3):
                act(xs[i] + y)

    def greet(target):
        pl.semaphore_signal(barrier, inc=1, device_id=target, device_id_type=MESH)

    mine = [
        pltpu.make_async_copy(f_hbm, f_in, in_sem.at[0]),
        pltpu.make_async_copy(
            w_hbm.at[gx // 8, pl.ds(3 * lax.rem(gx, 8), 3)], w_in, in_sem.at[1]
        ),
        pltpu.make_async_copy(pw_hbm, pw_in, in_sem.at[2]),
        pltpu.make_async_copy(bias_hbm, bias_in, in_sem.at[3]),
        pltpu.make_async_copy(cw_hbm, cw_in, in_sem.at[4]),
    ]
    loads = [
        pltpu.make_async_copy(tables_hbm[i], tables[i], table_sem.at[i]) for i in range(TABLES)
    ]
    loads[0].start()
    mine[0].start()

    at_y = lax.rem(gx, 4)
    x_mates = [xs[i] + at_y for i in range(3)]
    for mate in x_mates:
        greet((mate, gy))
    for k in (2, 1, 3):
        greet((gx - at_y + lax.rem(at_y + k, 4), gy))
    each_gy(lambda to: greet((gx, to)))
    sides = [(dx, dy) for dx in (-1, 0, 1) for dy in (-1, 0, 1) if (dx, dy) != (0, 0)]

    def beside(dx, dy):
        return (lax.rem(gx + dx + GX, GX), lax.rem(gy + dy + GY, GY))

    for dx, dy in sides:
        if dx != 0 and dy != 0:
            greet(beside(dx, dy))
    for load in loads[1:]:
        load.start()
    for load in mine[1:]:
        load.start()

    mine[0].wait()
    loads[0].wait()
    f_rows[...] = f_in.reshape(ROWS, DEPTH)[...]
    hat = mm_nt(t_zf[...], f_rows[...]).astype(BF)
    for m in range(2):
        send_one[m] = hat[m * MODES : (m + 1) * MODES].reshape(GY, 2, ROWS)

    def along_gy(at, source, target):
        own = pltpu.make_async_copy(source.at[gy], target.at[gy], recv_sem.at[at])
        own.start()

        def send(to):
            pltpu.make_async_remote_copy(
                src_ref=source.at[to],
                dst_ref=target.at[gy],
                send_sem=send_sem.at[at],
                recv_sem=recv_sem.at[at],
                device_id=(gx, to),
                device_id_type=MESH,
            ).start()

        each_gy(send)

    def arrived(at, whole):
        pltpu.make_async_copy(whole, whole, recv_sem.at[at]).wait()

    def left(at, source, count):
        part = source.at[pl.ds(0, count)]
        pltpu.make_async_copy(part, part, send_sem.at[at]).wait()

    pl.semaphore_wait(barrier, (GY - 1) + 6 + 4)
    for m in range(2):
        along_gy(m, send_one.at[m], recv_one.at[m])
    for mate in x_mates:
        pl.semaphore_signal(heard, inc=1, device_id=(mate, gy), device_id_type=MESH)

    for i in (8, 9):
        loads[i].wait()
    for pair in range(LX // 2):
        rows = mm(t_pair_pool[...], f_rows[pair * PAIR : (pair + 1) * PAIR])
        high, low = halves(rows)
        cells = mm(high, t_lane_pool[...]) + mm(low, t_lane_pool[...])
        pool[pair + 1, 1:3] = cells.astype(BF).reshape(2, 9, 2, HALF)

    def rim(which, dx, dy):
        sx = {-1: pl.ds(1, 1), 0: pl.ds(1, 4), 1: pl.ds(4, 1)}[dx]
        tx = {-1: pl.ds(5, 1), 0: pl.ds(1, 4), 1: pl.ds(0, 1)}[dx]
        sy = {-1: pl.ds(1, 1), 0: pl.ds(1, 2), 1: pl.ds(2, 1)}[dy]
        ty = {-1: pl.ds(3, 1), 0: pl.ds(1, 2), 1: pl.ds(0, 1)}[dy]
        return pltpu.make_async_remote_copy(
            src_ref=pool.at[sx, sy],
            dst_ref=pool.at[tx, ty],
            send_sem=halo_send.at[which],
            recv_sem=halo_recv.at[which],
            device_id=beside(dx, dy),
            device_id_type=MESH,
        )

    rims = [rim(i, dx, dy) for i, (dx, dy) in enumerate(sides)]

    w_wide[...] = jnp.zeros_like(w_wide)
    mine[1].wait()

    def widen(at, _):
        value = w_in.reshape(3 * CH, CH, 2, MX)[at].astype(FLT).reshape(2 * CH, MX)
        for u in range(4):
            w_wide[at, 0 : 2 * CH, u * SLOT : u * SLOT + MX] = value
        return 0

    lax.fori_loop(0, 3 * CH, widen, 0)

    for i in (1, 2):
        loads[i].wait()
    lane = lax.rem(lax.broadcasted_iota(jnp.int32, (8 * JS, ROWS), 1), LY)
    for m in range(2):
        arrived(m, recv_one.at[m])
        part = mm(t_y[...], recv_one[m].reshape(2 * GY, ROWS)).reshape(LY, 8 * JS, ROWS)
        chosen = part[0]
        for y in range(1, LY):
            chosen = jnp.where(lane == y, part[y], chosen)
        both = mm(jnp.concatenate(halves(chosen), axis=0), t_gather[...])
        second = both[: 8 * JS] + both[8 * JS :]
        second = [second[:, h * 128 : (h + 1) * 128].reshape(8, JS, 128) for h in range(2)]
        send_two[8 * m : 8 * m + 8] = jnp.concatenate(second, axis=1).astype(BF)

        if m == 0:
            pl.semaphore_wait(heard, 3)
        for k in far:
            y = lax.rem(lax.rem(gx, 4) + k, 4)
            for x in (2 * m, 2 * m + 1):
                to = 4 * x + y

                @pl.when(to != gx)
                def _(to=to):
                    pltpu.make_async_remote_copy(
                        src_ref=send_two.at[to],
                        dst_ref=recv_two.at[gx],
                        send_sem=send_sem.at[2],
                        recv_sem=recv_sem.at[2],
                        device_id=(to, gy),
                        device_id_type=MESH,
                    ).start()

    pltpu.make_async_copy(send_two.at[gx], recv_two.at[gx], recv_sem.at[2]).start()
    for copy in rims:
        copy.start()

    for i in (3, 4):
        loads[i].wait()
    arrived(2, recv_two)
    turned = mm_tn(recv_two[...].reshape(GX * 2 * JS, 128), t_x[...])
    group = lax.broadcasted_iota(jnp.int32, (SLOT, 128), 1) // SLOT
    for at in range(6):
        acc = jnp.zeros((SLOT, 128), FLT)
        for u in range(4):
            piece = turned[u * SLOT : (u + 1) * SLOT, at * 128 : (at + 1) * 128]
            acc = acc + jnp.where(group == u, piece, 0.0)
        acc = acc + pltpu.roll(acc, 64, 1)
        acc = acc + pltpu.roll(acc, 32, 1)
        third[at] = acc

    blocks = []
    for j in range(3):
        real = jnp.zeros((24, 128), FLT)
        imag = jnp.zeros((24, 128), FLT)
        for c in range(CH):
            w_real = w_wide[j * CH + c, pl.ds(0, 24, stride=2), :]
            w_imag = w_wide[j * CH + c, pl.ds(1, 24, stride=2), :]
            u_real = third[2 * j, c : c + 1, :]
            u_imag = third[2 * j + 1, c : c + 1, :]
            real = real + (w_real * u_real - w_imag * u_imag)
            imag = imag + (w_real * u_imag + w_imag * u_real)
        for value in (real, imag):
            tall = []
            for u in range(4):
                tall += [jnp.where(group[:24] == u, value, 0.0), jnp.zeros((8, 128), FLT)]
            blocks.append(jnp.concatenate(tall, axis=0).astype(BF))
    back = mm_nt(t_ix[...], jnp.concatenate(blocks, axis=1))
    send_three[...] = back.astype(BF).reshape(GX, 2 * JS, 128)
    at_three = 3 + lax.div(gx, 8)
    pltpu.make_async_copy(send_three.at[gx], recv_three.at[gx], recv_sem.at[at_three]).start()

    def send(to):
        pltpu.make_async_remote_copy(
            src_ref=send_three.at[to],
            dst_ref=recv_three.at[gx],
            send_sem=send_sem.at[3],
            recv_sem=recv_sem.at[at_three],
            device_id=(to, gy),
            device_id_type=MESH,
        ).start()

    each_gx(send)

    for i in (2, 3, 4):
        mine[i].wait()
    for i in range(10, TABLES):
        loads[i].wait()
    wide = mm_nt(t_spread_o[...], pw_in[...]).astype(BF)
    wide = mm_nt(wide, t_spread_o[...]).astype(BF)
    point[...] = wide * t_same[...]
    taps[...] = jnp.zeros_like(taps)
    for c in range(CH):
        taps[c, 0:CH, 0:27] = cw_in[c].astype(FLT)
    flat = taps[...].reshape(24 * CH, 128).astype(BF)
    for at in range(6):
        placed = mm(flat, t_conv_place[at]).astype(BF) * t_conv_same[...]
        conv[at * 24 : (at + 1) * 24] = mm(t_conv_sum[...], placed)

    for copy in rims:
        copy.wait_recv()

    @pl.when(gx == 0)
    def _():
        pool[0] = jnp.zeros((4, 9, 2, HALF), BF)

    @pl.when(gx == GX - 1)
    def _():
        pool[5] = jnp.zeros((4, 9, 2, HALF), BF)

    @pl.when(gy == 0)
    def _():
        pool[:, 0] = jnp.zeros((6, 9, 2, HALF), BF)

    @pl.when(gy == GY - 1)
    def _():
        pool[:, 3] = jnp.zeros((6, 9, 2, HALF), BF)

    for i in (5, 6, 7):
        loads[i].wait()
    for m in range(2):
        mine_three = recv_three.at[pl.ds(8 * m, 8)]
        arrived(3 + m, mine_three)
        wide_in = mine_three[...].astype(FLT)
        sides_in = [wide_in[:, h * JS : (h + 1) * JS].reshape(8 * JS, 128) for h in range(2)]
        spread = mm(jnp.concatenate(sides_in, axis=1).astype(BF), t_spread[...]).astype(BF)
        part = mm(t_iy[...], spread).reshape(LY, 2 * GY, ROWS)
        chosen = part[0]
        for y in range(1, LY):
            chosen = jnp.where(lane == y, part[y], chosen)
        send_four[m] = chosen.astype(BF).reshape(GY, 2, ROWS)
        along_gy(5 + m, send_four.at[m], recv_four.at[m])

    column = jnp.sum(t_spread_o[...].astype(FLT) * bias_in[...], axis=1, keepdims=True)
    spot = lax.broadcasted_iota(jnp.int32, (48, HALF), 1)
    conv_matrix = conv[...].astype(BF)
    for pair in range(LX // 2):
        sums = mm(conv_matrix, pool[pair : pair + 3].reshape(12 * CH, HALF))
        below = jnp.where(spot >= STEPS, pltpu.roll(sums[0:48], STEPS, 1), 0.0)
        above = jnp.where(spot < HALF - STEPS, pltpu.roll(sums[96:144], HALF - STEPS, 1), 0.0)
        high, low = halves(jax.nn.gelu(sums[48:96] + below + above))
        span = slice(pair * PAIR, (pair + 1) * PAIR)
        up = mm(t_row_up[...], mm(high, t_lane_up[...]).astype(BF))
        up = up + mm(t_row_up[...], mm(low, t_lane_up[...]).astype(BF))
        base[span] = mm(point[...], f_rows[span]) + up + column

    arrived(5, recv_four.at[0])
    columns = recv_four[0].reshape(2 * GY, ROWS).astype(FLT).T.astype(BF)
    for pair in range(LX // 2):
        span = slice(pair * PAIR, (pair + 1) * PAIR)
        base[span] += mm(columns[span], t_zi[0])
    arrived(6, recv_four.at[1])
    columns = recv_four[1].reshape(2 * GY, ROWS).astype(FLT).T.astype(BF)
    for pair in range(LX // 2):
        span = slice(pair * PAIR, (pair + 1) * PAIR)
        total = mm(columns[span], t_zi[1]) + base[span]
        out_ref[pair * 36 : (pair + 1) * 36] = jax.nn.gelu(total).astype(BF).reshape(36, 4, DEPTH)
    for m in range(2):
        left(m, send_one.at[m], GY - 1)
        left(5 + m, send_four.at[m], GY - 1)
    left(2, send_two, GX - 1)
    left(3, send_three, GX - 1)
    for copy in rims:
        copy.wait_send()


def local(features, mode_weights, point_weight, bias_term, conv_weight):
    tables = make_tables()
    f = features.transpose(0, 2, 1, 3).reshape(LX * CH, LY, DEPTH)
    w = mode_weights.transpose(0, 1, 3, 4, 2, 5)
    taps = conv_weight.transpose(1, 2, 0)
    operands = [f, w, point_weight, bias_term.reshape(1, CH), taps]
    vmem = [
        pltpu.VMEM(f.shape, BF),
        pltpu.VMEM((3,) + w.shape[2:], BF),
        pltpu.VMEM(point_weight.shape, BF),
        pltpu.VMEM((1, CH), FLT),
        pltpu.VMEM(taps.shape, BF),
    ]
    vmem += [pltpu.VMEM(t.shape, BF) for t in tables]
    vmem += [
        pltpu.VMEM((ROWS, DEPTH), BF),
        pltpu.VMEM((2, GY, 2, ROWS), BF),
        pltpu.VMEM((2, GY, 2, ROWS), BF),
        pltpu.VMEM((GX, 2 * JS, 128), BF),
        pltpu.VMEM((GX, 2 * JS, 128), BF),
        pltpu.VMEM((GX, 2 * JS, 128), BF),
        pltpu.VMEM((GX, 2 * JS, 128), BF),
        pltpu.VMEM((2, GY, 2, ROWS), BF),
        pltpu.VMEM((2, GY, 2, ROWS), BF),
        pltpu.VMEM((6, 4, 9, 2, HALF), BF),
        pltpu.VMEM((PAIR, PAIR), BF),
        pltpu.VMEM((CH, 24, 128), FLT),
        pltpu.VMEM((144, 12 * CH), FLT),
        pltpu.VMEM((3 * CH, 48, 128), FLT),
        pltpu.VMEM((6, SLOT, 128), FLT),
        pltpu.VMEM((ROWS, DEPTH), FLT),
        pltpu.SemaphoreType.DMA((5,)),
        pltpu.SemaphoreType.DMA((TABLES,)),
        pltpu.SemaphoreType.DMA((7,)),
        pltpu.SemaphoreType.DMA((7,)),
        pltpu.SemaphoreType.DMA((8,)),
        pltpu.SemaphoreType.DMA((8,)),
        pltpu.SemaphoreType.REGULAR,
    ]
    out = pl.pallas_call(
        kernel,
        out_shape=jax.ShapeDtypeStruct(f.shape, BF),
        in_specs=[pl.BlockSpec(memory_space=pltpu.HBM)] * (5 + len(tables)),
        out_specs=pl.BlockSpec(memory_space=pltpu.VMEM),
        scratch_shapes=vmem,
        compiler_params=pltpu.CompilerParams(
            collective_id=0, has_side_effects=True, vmem_limit_bytes=48 << 20
        ),
        name="layer",
    )(*[pltpu.with_memory_space_constraint(t, pltpu.HBM) for t in operands + [jnp.asarray(t) for t in tables]])
    return out.reshape(LX, CH, LY, DEPTH).transpose(0, 2, 1, 3)


def solution(mesh):
    in_specs = (P("gx", "gy", None, None), P("gy", None, None, None, None, None), P(), P(), P())
    out_specs = P("gx", "gy", None, None)
    return jax.shard_map(local, mesh=mesh, in_specs=in_specs, out_specs=out_specs, check_vma=False)
```

```python
import math

import jax
import jax.numpy as jnp
import ml_dtypes
import numpy as np
from jax import lax
from jax.experimental import pallas as pl
from jax.experimental.pallas import tpu as pltpu
from jax.sharding import PartitionSpec as P

BF = jnp.bfloat16
FLT = jnp.float32
MESH = pl.DeviceIdType.MESH

GRID_Z, STEPS, CH = 64, 8, 18
MX, MY, MZ, MT = 24, 24, 16, 4
GX, GY = 16, 32
LX, LY = 8, 4
ROWS = LX * CH * LY
PAIR = 2 * CH * LY
DEPTH = GRID_Z * STEPS
HALF = DEPTH // 2
MODES = MZ * MT
JS = 8
SLOT = 32
TABLES = 17


def frequencies(number):
    places = np.arange(number, dtype=np.int32)
    return np.where(places < number // 2, places, places - number)


def angles_of(number, length):
    places = np.arange(length, dtype=np.int32)
    fraction = np.mod(frequencies(number)[:, None] * places[None, :], length).astype(np.float32)
    return np.float32(2.0 * math.pi) * (fraction / np.float32(length))


def rounded(table):
    return np.asarray(table, np.float32).astype(ml_dtypes.bfloat16).astype(np.float32)


def forward_table(number, length):
    angles = angles_of(number, length).T
    cosine = np.cos(angles) / np.float32(math.sqrt(length))
    sine = np.sin(angles) / np.float32(math.sqrt(length))
    return rounded(np.stack([np.stack([cosine, -sine], 1), np.stack([sine, cosine], 1)], 0))


def inverse_table(number, length):
    angles = angles_of(number, length)
    cosine = np.cos(angles) / np.float32(math.sqrt(number))
    sine = np.sin(angles) / np.float32(math.sqrt(number))
    return rounded(np.stack([np.stack([cosine, sine], 1), np.stack([-sine, cosine], 1)], 0))


def depth_tables():
    along_z = angles_of(MZ, GRID_Z)
    time_freq = np.arange(MT, dtype=np.int32)
    time_pos = np.arange(STEPS, dtype=np.int32)
    along_t = np.mod(time_freq[:, None] * time_pos[None, :], STEPS).astype(np.float32)
    along_t = np.float32(2.0 * math.pi) * along_t / np.float32(STEPS)
    angles = along_z[:, None, :, None] + along_t[None, :, None, :]
    cosine, sine = np.cos(angles), np.sin(angles)
    forward = np.stack([cosine, -sine], 2) / np.float32(math.sqrt(DEPTH))
    forward = forward.reshape(2 * MODES, DEPTH)
    factor = np.where(time_freq == 0, 1.0, 2.0).astype(np.float32)[None, :, None, None]
    factor = factor / np.float32(math.sqrt(MODES))
    inverse = np.stack([factor * cosine, -factor * sine], 2).reshape(2 * MODES, DEPTH)
    return rounded(forward), rounded(inverse)


def make_tables():
    zt_forward, zt_inverse = depth_tables()
    yf, yi = forward_table(MY, GY * LY), inverse_table(MY, GY * LY)
    xf, xi = forward_table(MX, GX * LX), inverse_table(MX, GX * LX)
    per = MY // 8
    block = yf.reshape(2, GY, LY, 2, 8, per)
    ty = np.zeros((LY, 8, JS, GY, 2), np.float32)
    ty[:, :, : 2 * per] = np.einsum("rgysaj->yajsgr", block).reshape(LY, 8, 2 * per, GY, 2)
    ty = ty.reshape(LY * 8 * JS, GY * 2)
    eyex, eyec, eyey = np.eye(LX), np.eye(CH, SLOT), np.eye(LY)
    gather = np.einsum("xX,cC,y->xcyXC", eyex, eyec, np.ones(LY)).reshape(ROWS, LX * SLOT)
    block = xf.reshape(2, GX, 2, 4, 2, MX)
    eyej = np.eye(per)
    tx = np.zeros((GX, 2, JS, per, 2, 4, SLOT), np.float32)
    tx[:, :, : 2 * per, :, :, :, :MX] = np.einsum("rahusk,ij->ahirjsuk", block, eyej).reshape(
        GX, 2, 2 * per, per, 2, 4, MX
    )
    tx = tx.reshape(GX * 2 * JS, per * 2 * 4 * SLOT)
    block = xi.reshape(2, MX, 2, GX, 2, 4)
    tix = np.zeros((GX, 2, JS, per, 2, 4, SLOT), np.float32)
    tix[:, :, : 2 * per, :, :, :, :MX] = np.einsum("rksahu,ij->ahisjruk", block, eyej).reshape(
        GX, 2, 2 * per, per, 2, 4, MX
    )
    tix = tix.reshape(GX * 2 * JS, per * 2 * 4 * SLOT)
    block = yi.reshape(2, 8, per, 2, GY, LY)
    tiy = np.zeros((LY, GY, 2, 8, JS), np.float32)
    tiy[..., : 2 * per] = np.einsum("rajsgy->ygsajr", block).reshape(LY, GY, 2, 8, 2 * per)
    tiy = tiy.reshape(LY * GY * 2, 8 * JS)
    zt_forward = zt_forward.reshape(GY, 2, 2, DEPTH).transpose(1, 0, 2, 3).reshape(2 * MODES, DEPTH)
    zt_inverse = zt_inverse.reshape(GY, 2, 2, DEPTH).transpose(1, 0, 2, 3).reshape(2, MODES, DEPTH)
    pair_pool = np.einsum("x,cC,yY->YCxcy", np.ones(2), np.eye(CH), np.repeat(np.eye(2), 2, 0))
    pair_pool = pair_pool.reshape(2 * CH, PAIR)
    lane_up = np.einsum("zZ,tT->ZTzt", np.repeat(np.eye(GRID_Z // 2), 2, 0), np.eye(STEPS))
    lane_up = lane_up.reshape(HALF, DEPTH)
    lane_pool = 0.125 * lane_up.T
    row_up = np.zeros((PAIR, 2, 24), np.float32)
    row_up[:, :, :CH] = pair_pool.T.reshape(PAIR, 2, CH)
    row_up = row_up.reshape(PAIR, 48)
    spread_o = np.einsum("x,oO,y->xoyO", np.ones(2), np.eye(CH), np.ones(LY)).reshape(PAIR, CH)
    same = np.einsum("xX,oc,yY->xoyXcY", np.eye(2), np.ones((CH, CH)), eyey).reshape(PAIR, PAIR)
    eyecc = np.eye(CH, dtype=np.float32)
    conv_place = np.zeros((3, 2, 128, 3, 4, CH), np.float32)
    for dx in range(3):
        for dy in range(3):
            for dz in range(3):
                for at in range(2):
                    conv_place[dz, at, 9 * dx + 3 * dy + dz, dx, dy + at] = 1.0
    conv_place = conv_place.reshape(6, 128, 12 * CH)
    conv_same = np.einsum("cC,o,d->coCd", eyecc, np.ones(24), np.ones(12))
    conv_same = conv_same.transpose(0, 1, 3, 2).reshape(24 * CH, 12 * CH)
    conv_sum = np.einsum("c,oO->ocO", np.ones(CH), np.eye(24)).reshape(24, 24 * CH)
    return [
        np.asarray(t, np.float32).astype(ml_dtypes.bfloat16)
        for t in (
            zt_forward,
            ty,
            gather,
            tx,
            tix,
            gather.T,
            tiy,
            zt_inverse,
            pair_pool,
            lane_pool,
            lane_up,
            row_up,
            spread_o,
            same,
            conv_place,
            conv_same,
            conv_sum,
        )
    ]


def mm(a, b):
    return jnp.dot(a, b, preferred_element_type=FLT)


def mm_nt(a, b):
    return lax.dot_general(a, b, (((1,), (1,)), ((), ())), preferred_element_type=FLT)


def mm_tn(a, b):
    return lax.dot_general(a, b, (((0,), (0,)), ((), ())), preferred_element_type=FLT)


def halves(value):
    high = value.astype(BF)
    return high, (value - high.astype(FLT)).astype(BF)


def kernel(*refs):
    (f_hbm, w_hbm, pw_hbm, bias_hbm, cw_hbm), refs = refs[:5], refs[5:]
    tables_hbm, refs = refs[:TABLES], refs[TABLES:]
    out_ref, refs = refs[0], refs[1:]
    (f_in, w_in, pw_in, bias_in, cw_in), refs = refs[:5], refs[5:]
    tables, refs = refs[:TABLES], refs[TABLES:]
    (
        f_rows,
        send_one,
        recv_one,
        send_two,
        recv_two,
        send_three,
        recv_three,
        send_four,
        recv_four,
        pool,
        point,
        taps,
        conv,
        w_wide,
        third,
        base,
        in_sem,
        table_sem,
        send_sem,
        recv_sem,
        halo_send,
        halo_recv,
        heard,
    ) = refs
    (
        t_zf,
        t_y,
        t_gather,
        t_x,
        t_ix,
        t_spread,
        t_iy,
        t_zi,
        t_pair_pool,
        t_lane_pool,
        t_lane_up,
        t_row_up,
        t_spread_o,
        t_same,
        t_conv_place,
        t_conv_same,
        t_conv_sum,
    ) = tables
    gx = lax.axis_index("gx")
    gy = lax.axis_index("gy")
    barrier = pltpu.get_barrier_semaphore()

    far = (2, 1, 3, 0)
    inner = lax.rem(gy, 4)
    lows = [lax.rem(inner + k, 4) for k in far]
    xs = [4 * lax.rem(lax.div(gx, 4) + k, 4) for k in far]

    planes = [4 * lax.rem(lax.div(gy, 4) + k, 8) for k in range(1, 8)]

    def each_gy(act):
        for step in (4, 3, 5, 2, 6, 1, 7):
            plane = planes[step - 1]
            for k in range(4):
                act(plane + lows[k])
        for k in range(3):
            act(gy - inner + lows[k])

    def each_gx(act):
        for k in far:
            y = lax.rem(lax.rem(gx, 4) + k, 4)
            for i in range(4 if k else 3):
                act(xs[i] + y)

    def greet(target):
        pl.semaphore_signal(barrier, inc=1, device_id=target, device_id_type=MESH)

    mine = [
        pltpu.make_async_copy(f_hbm, f_in, in_sem.at[0]),
        pltpu.make_async_copy(
            w_hbm.at[gx // 8, pl.ds(3 * lax.rem(gx, 8), 3)], w_in, in_sem.at[1]
        ),
        pltpu.make_async_copy(pw_hbm, pw_in, in_sem.at[2]),
        pltpu.make_async_copy(bias_hbm, bias_in, in_sem.at[3]),
        pltpu.make_async_copy(cw_hbm, cw_in, in_sem.at[4]),
    ]
    loads = [
        pltpu.make_async_copy(tables_hbm[i], tables[i], table_sem.at[i]) for i in range(TABLES)
    ]
    loads[0].start()
    mine[0].start()

    each_gy(lambda to: greet((gx, to)))
    at_y = lax.rem(gx, 4)
    x_mates = [xs[i] + at_y for i in range(3)]
    for mate in x_mates:
        greet((mate, gy))
    for k in (2, 1, 3):
        greet((gx - at_y + lax.rem(at_y + k, 4), gy))
    sides = [(dx, dy) for dx in (-1, 0, 1) for dy in (-1, 0, 1) if (dx, dy) != (0, 0)]

    def beside(dx, dy):
        return (lax.rem(gx + dx + GX, GX), lax.rem(gy + dy + GY, GY))

    for dx, dy in sides:
        if dx != 0 and dy != 0:
            greet(beside(dx, dy))
    for load in loads[1:]:
        load.start()
    for load in mine[1:]:
        load.start()

    mine[0].wait()
    loads[0].wait()
    f_rows[...] = f_in.reshape(ROWS, DEPTH)[...]
    hat = mm_nt(t_zf[...], f_rows[...]).astype(BF)
    for m in range(2):
        send_one[m] = hat[m * MODES : (m + 1) * MODES].reshape(GY, 2, ROWS)

    def along_gy(at, source, target):
        own = pltpu.make_async_copy(source.at[gy], target.at[gy], recv_sem.at[at])
        own.start()

        def send(to):
            pltpu.make_async_remote_copy(
                src_ref=source.at[to],
                dst_ref=target.at[gy],
                send_sem=send_sem.at[at],
                recv_sem=recv_sem.at[at],
                device_id=(gx, to),
                device_id_type=MESH,
            ).start()

        each_gy(send)

    def arrived(at, whole):
        pltpu.make_async_copy(whole, whole, recv_sem.at[at]).wait()

    def left(at, source, count):
        part = source.at[pl.ds(0, count)]
        pltpu.make_async_copy(part, part, send_sem.at[at]).wait()

    pl.semaphore_wait(barrier, (GY - 1) + 6 + 4)
    for m in range(2):
        along_gy(m, send_one.at[m], recv_one.at[m])
    for mate in x_mates:
        pl.semaphore_signal(heard, inc=1, device_id=(mate, gy), device_id_type=MESH)

    def rim(which, dx, dy):
        sx = {-1: pl.ds(1, 1), 0: pl.ds(1, 4), 1: pl.ds(4, 1)}[dx]
        tx = {-1: pl.ds(5, 1), 0: pl.ds(1, 4), 1: pl.ds(0, 1)}[dx]
        sy = {-1: pl.ds(1, 1), 0: pl.ds(1, 2), 1: pl.ds(2, 1)}[dy]
        ty = {-1: pl.ds(3, 1), 0: pl.ds(1, 2), 1: pl.ds(0, 1)}[dy]
        return pltpu.make_async_remote_copy(
            src_ref=pool.at[sx, sy],
            dst_ref=pool.at[tx, ty],
            send_sem=halo_send.at[which],
            recv_sem=halo_recv.at[which],
            device_id=beside(dx, dy),
            device_id_type=MESH,
        )

    rims = [rim(i, dx, dy) for i, (dx, dy) in enumerate(sides)]

    w_wide[...] = jnp.zeros_like(w_wide)
    mine[1].wait()

    def widen(at, _):
        value = w_in.reshape(3 * CH, CH, 2, MX)[at].astype(FLT).reshape(2 * CH, MX)
        for u in range(4):
            w_wide[at, 0 : 2 * CH, u * SLOT : u * SLOT + MX] = value
        return 0

    lax.fori_loop(0, 3 * CH, widen, 0)

    for i in (1, 2):
        loads[i].wait()
    lane = lax.rem(lax.broadcasted_iota(jnp.int32, (8 * JS, ROWS), 1), LY)
    for m in range(2):
        arrived(m, recv_one.at[m])
        part = mm(t_y[...], recv_one[m].reshape(2 * GY, ROWS)).reshape(LY, 8 * JS, ROWS)
        chosen = part[0]
        for y in range(1, LY):
            chosen = jnp.where(lane == y, part[y], chosen)
        both = mm(jnp.concatenate(halves(chosen), axis=0), t_gather[...])
        second = both[: 8 * JS] + both[8 * JS :]
        second = [second[:, h * 128 : (h + 1) * 128].reshape(8, JS, 128) for h in range(2)]
        send_two[8 * m : 8 * m + 8] = jnp.concatenate(second, axis=1).astype(BF)

        if m == 0:
            pl.semaphore_wait(heard, 3)
        for k in far:
            y = lax.rem(lax.rem(gx, 4) + k, 4)
            for x in (2 * m, 2 * m + 1):
                to = 4 * x + y

                @pl.when(to != gx)
                def _(to=to):
                    pltpu.make_async_remote_copy(
                        src_ref=send_two.at[to],
                        dst_ref=recv_two.at[gx],
                        send_sem=send_sem.at[2],
                        recv_sem=recv_sem.at[2],
                        device_id=(to, gy),
                        device_id_type=MESH,
                    ).start()

    pltpu.make_async_copy(send_two.at[gx], recv_two.at[gx], recv_sem.at[2]).start()
    for i in (8, 9):
        loads[i].wait()
    for pair in range(LX // 2):
        rows = mm(t_pair_pool[...], f_rows[pair * PAIR : (pair + 1) * PAIR])
        high, low = halves(rows)
        cells = mm(high, t_lane_pool[...]) + mm(low, t_lane_pool[...])
        pool[pair + 1, 1:3] = cells.astype(BF).reshape(2, 9, 2, HALF)

    for copy in rims:
        copy.start()

    for i in (3, 4):
        loads[i].wait()
    arrived(2, recv_two)
    turned = mm_tn(recv_two[...].reshape(GX * 2 * JS, 128), t_x[...])
    group = lax.broadcasted_iota(jnp.int32, (SLOT, 128), 1) // SLOT
    for at in range(6):
        acc = jnp.zeros((SLOT, 128), FLT)
        for u in range(4):
            piece = turned[u * SLOT : (u + 1) * SLOT, at * 128 : (at + 1) * 128]
            acc = acc + jnp.where(group == u, piece, 0.0)
        acc = acc + pltpu.roll(acc, 64, 1)
        acc = acc + pltpu.roll(acc, 32, 1)
        third[at] = acc

    blocks = []
    for j in range(3):
        real = jnp.zeros((24, 128), FLT)
        imag = jnp.zeros((24, 128), FLT)
        for c in range(CH):
            w_real = w_wide[j * CH + c, pl.ds(0, 24, stride=2), :]
            w_imag = w_wide[j * CH + c, pl.ds(1, 24, stride=2), :]
            u_real = third[2 * j, c : c + 1, :]
            u_imag = third[2 * j + 1, c : c + 1, :]
            real = real + (w_real * u_real - w_imag * u_imag)
            imag = imag + (w_real * u_imag + w_imag * u_real)
        for value in (real, imag):
            tall = []
            for u in range(4):
                tall += [jnp.where(group[:24] == u, value, 0.0), jnp.zeros((8, 128), FLT)]
            blocks.append(jnp.concatenate(tall, axis=0).astype(BF))
    back = mm_nt(t_ix[...], jnp.concatenate(blocks, axis=1))
    send_three[...] = back.astype(BF).reshape(GX, 2 * JS, 128)
    at_three = 3 + lax.div(gx, 8)
    pltpu.make_async_copy(send_three.at[gx], recv_three.at[gx], recv_sem.at[at_three]).start()

    def send(to):
        pltpu.make_async_remote_copy(
            src_ref=send_three.at[to],
            dst_ref=recv_three.at[gx],
            send_sem=send_sem.at[3],
            recv_sem=recv_sem.at[at_three],
            device_id=(to, gy),
            device_id_type=MESH,
        ).start()

    each_gx(send)

    for i in (2, 3, 4):
        mine[i].wait()
    for i in range(10, TABLES):
        loads[i].wait()
    wide = mm_nt(t_spread_o[...], pw_in[...]).astype(BF)
    wide = mm_nt(wide, t_spread_o[...]).astype(BF)
    point[...] = wide * t_same[...]
    taps[...] = jnp.zeros_like(taps)
    for c in range(CH):
        taps[c, 0:CH, 0:27] = cw_in[c].astype(FLT)
    flat = taps[...].reshape(24 * CH, 128).astype(BF)
    for at in range(6):
        placed = mm(flat, t_conv_place[at]).astype(BF) * t_conv_same[...]
        conv[at * 24 : (at + 1) * 24] = mm(t_conv_sum[...], placed)

    for copy in rims:
        copy.wait_recv()

    @pl.when(gx == 0)
    def _():
        pool[0] = jnp.zeros((4, 9, 2, HALF), BF)

    @pl.when(gx == GX - 1)
    def _():
        pool[5] = jnp.zeros((4, 9, 2, HALF), BF)

    @pl.when(gy == 0)
    def _():
        pool[:, 0] = jnp.zeros((6, 9, 2, HALF), BF)

    @pl.when(gy == GY - 1)
    def _():
        pool[:, 3] = jnp.zeros((6, 9, 2, HALF), BF)

    for i in (5, 6, 7):
        loads[i].wait()
    for m in range(2):
        mine_three = recv_three.at[pl.ds(8 * m, 8)]
        arrived(3 + m, mine_three)
        wide_in = mine_three[...].astype(FLT)
        sides_in = [wide_in[:, h * JS : (h + 1) * JS].reshape(8 * JS, 128) for h in range(2)]
        spread = mm(jnp.concatenate(sides_in, axis=1).astype(BF), t_spread[...]).astype(BF)
        part = mm(t_iy[...], spread).reshape(LY, 2 * GY, ROWS)
        chosen = part[0]
        for y in range(1, LY):
            chosen = jnp.where(lane == y, part[y], chosen)
        send_four[m] = chosen.astype(BF).reshape(GY, 2, ROWS)
        along_gy(5 + m, send_four.at[m], recv_four.at[m])

    column = jnp.sum(t_spread_o[...].astype(FLT) * bias_in[...], axis=1, keepdims=True)
    spot = lax.broadcasted_iota(jnp.int32, (48, HALF), 1)
    conv_matrix = conv[...].astype(BF)
    for pair in range(LX // 2):
        sums = mm(conv_matrix, pool[pair : pair + 3].reshape(12 * CH, HALF))
        below = jnp.where(spot >= STEPS, pltpu.roll(sums[0:48], STEPS, 1), 0.0)
        above = jnp.where(spot < HALF - STEPS, pltpu.roll(sums[96:144], HALF - STEPS, 1), 0.0)
        high, low = halves(jax.nn.gelu(sums[48:96] + below + above))
        span = slice(pair * PAIR, (pair + 1) * PAIR)
        up = mm(t_row_up[...], mm(high, t_lane_up[...]).astype(BF))
        up = up + mm(t_row_up[...], mm(low, t_lane_up[...]).astype(BF))
        base[span] = mm(point[...], f_rows[span]) + up + column

    arrived(5, recv_four.at[0])
    columns = recv_four[0].reshape(2 * GY, ROWS).astype(FLT).T.astype(BF)
    for pair in range(LX // 2):
        span = slice(pair * PAIR, (pair + 1) * PAIR)
        base[span] += mm(columns[span], t_zi[0])
    arrived(6, recv_four.at[1])
    columns = recv_four[1].reshape(2 * GY, ROWS).astype(FLT).T.astype(BF)
    for pair in range(LX // 2):
        span = slice(pair * PAIR, (pair + 1) * PAIR)
        total = mm(columns[span], t_zi[1]) + base[span]
        out_ref[pair * 36 : (pair + 1) * 36] = jax.nn.gelu(total).astype(BF).reshape(36, 4, DEPTH)
    for m in range(2):
        left(m, send_one.at[m], GY - 1)
        left(5 + m, send_four.at[m], GY - 1)
    left(2, send_two, GX - 1)
    left(3, send_three, GX - 1)
    for copy in rims:
        copy.wait_send()


def local(features, mode_weights, point_weight, bias_term, conv_weight):
    tables = make_tables()
    f = features.transpose(0, 2, 1, 3).reshape(LX * CH, LY, DEPTH)
    w = mode_weights.transpose(0, 1, 3, 4, 2, 5)
    taps = conv_weight.transpose(1, 2, 0)
    operands = [f, w, point_weight, bias_term.reshape(1, CH), taps]
    vmem = [
        pltpu.VMEM(f.shape, BF),
        pltpu.VMEM((3,) + w.shape[2:], BF),
        pltpu.VMEM(point_weight.shape, BF),
        pltpu.VMEM((1, CH), FLT),
        pltpu.VMEM(taps.shape, BF),
    ]
    vmem += [pltpu.VMEM(t.shape, BF) for t in tables]
    vmem += [
        pltpu.VMEM((ROWS, DEPTH), BF),
        pltpu.VMEM((2, GY, 2, ROWS), BF),
        pltpu.VMEM((2, GY, 2, ROWS), BF),
        pltpu.VMEM((GX, 2 * JS, 128), BF),
        pltpu.VMEM((GX, 2 * JS, 128), BF),
        pltpu.VMEM((GX, 2 * JS, 128), BF),
        pltpu.VMEM((GX, 2 * JS, 128), BF),
        pltpu.VMEM((2, GY, 2, ROWS), BF),
        pltpu.VMEM((2, GY, 2, ROWS), BF),
        pltpu.VMEM((6, 4, 9, 2, HALF), BF),
        pltpu.VMEM((PAIR, PAIR), BF),
        pltpu.VMEM((CH, 24, 128), FLT),
        pltpu.VMEM((144, 12 * CH), FLT),
        pltpu.VMEM((3 * CH, 48, 128), FLT),
        pltpu.VMEM((6, SLOT, 128), FLT),
        pltpu.VMEM((ROWS, DEPTH), FLT),
        pltpu.SemaphoreType.DMA((5,)),
        pltpu.SemaphoreType.DMA((TABLES,)),
        pltpu.SemaphoreType.DMA((7,)),
        pltpu.SemaphoreType.DMA((7,)),
        pltpu.SemaphoreType.DMA((8,)),
        pltpu.SemaphoreType.DMA((8,)),
        pltpu.SemaphoreType.REGULAR,
    ]
    out = pl.pallas_call(
        kernel,
        out_shape=jax.ShapeDtypeStruct(f.shape, BF),
        in_specs=[pl.BlockSpec(memory_space=pltpu.HBM)] * (5 + len(tables)),
        out_specs=pl.BlockSpec(memory_space=pltpu.VMEM),
        scratch_shapes=vmem,
        compiler_params=pltpu.CompilerParams(
            collective_id=0, has_side_effects=True, vmem_limit_bytes=48 << 20
        ),
        name="layer",
    )(*[pltpu.with_memory_space_constraint(t, pltpu.HBM) for t in operands + [jnp.asarray(t) for t in tables]])
    return out.reshape(LX, CH, LY, DEPTH).transpose(0, 2, 1, 3)


def solution(mesh):
    in_specs = (P("gx", "gy", None, None), P("gy", None, None, None, None, None), P(), P(), P())
    out_specs = P("gx", "gy", None, None)
    return jax.shard_map(local, mesh=mesh, in_specs=in_specs, out_specs=out_specs, check_vma=False)
```

```python
import math

import jax
import jax.numpy as jnp
import ml_dtypes
import numpy as np
from jax import lax
from jax.experimental import pallas as pl
from jax.experimental.pallas import tpu as pltpu
from jax.sharding import PartitionSpec as P

BF = jnp.bfloat16
FLT = jnp.float32
MESH = pl.DeviceIdType.MESH

GRID_Z, STEPS, CH = 64, 8, 18
MX, MY, MZ, MT = 24, 24, 16, 4
GX, GY = 16, 32
LX, LY = 8, 4
ROWS = LX * CH * LY
PAIR = 2 * CH * LY
DEPTH = GRID_Z * STEPS
HALF = DEPTH // 2
MODES = MZ * MT
JS = 8
SLOT = 32
TABLES = 17


def frequencies(number):
    places = np.arange(number, dtype=np.int32)
    return np.where(places < number // 2, places, places - number)


def angles_of(number, length):
    places = np.arange(length, dtype=np.int32)
    fraction = np.mod(frequencies(number)[:, None] * places[None, :], length).astype(np.float32)
    return np.float32(2.0 * math.pi) * (fraction / np.float32(length))


def rounded(table):
    return np.asarray(table, np.float32).astype(ml_dtypes.bfloat16).astype(np.float32)


def forward_table(number, length):
    angles = angles_of(number, length).T
    cosine = np.cos(angles) / np.float32(math.sqrt(length))
    sine = np.sin(angles) / np.float32(math.sqrt(length))
    return rounded(np.stack([np.stack([cosine, -sine], 1), np.stack([sine, cosine], 1)], 0))


def inverse_table(number, length):
    angles = angles_of(number, length)
    cosine = np.cos(angles) / np.float32(math.sqrt(number))
    sine = np.sin(angles) / np.float32(math.sqrt(number))
    return rounded(np.stack([np.stack([cosine, sine], 1), np.stack([-sine, cosine], 1)], 0))


def depth_tables():
    along_z = angles_of(MZ, GRID_Z)
    time_freq = np.arange(MT, dtype=np.int32)
    time_pos = np.arange(STEPS, dtype=np.int32)
    along_t = np.mod(time_freq[:, None] * time_pos[None, :], STEPS).astype(np.float32)
    along_t = np.float32(2.0 * math.pi) * along_t / np.float32(STEPS)
    angles = along_z[:, None, :, None] + along_t[None, :, None, :]
    cosine, sine = np.cos(angles), np.sin(angles)
    forward = np.stack([cosine, -sine], 2) / np.float32(math.sqrt(DEPTH))
    forward = forward.reshape(2 * MODES, DEPTH)
    factor = np.where(time_freq == 0, 1.0, 2.0).astype(np.float32)[None, :, None, None]
    factor = factor / np.float32(math.sqrt(MODES))
    inverse = np.stack([factor * cosine, -factor * sine], 2).reshape(2 * MODES, DEPTH)
    return rounded(forward), rounded(inverse)


def make_tables():
    zt_forward, zt_inverse = depth_tables()
    yf, yi = forward_table(MY, GY * LY), inverse_table(MY, GY * LY)
    xf, xi = forward_table(MX, GX * LX), inverse_table(MX, GX * LX)
    per = MY // 8
    block = yf.reshape(2, GY, LY, 2, 8, per)
    ty = np.zeros((LY, 8, JS, GY, 2), np.float32)
    ty[:, :, : 2 * per] = np.einsum("rgysaj->yajsgr", block).reshape(LY, 8, 2 * per, GY, 2)
    ty = ty.reshape(LY * 8 * JS, GY * 2)
    eyex, eyec, eyey = np.eye(LX), np.eye(CH, SLOT), np.eye(LY)
    gather = np.einsum("xX,cC,y->xcyXC", eyex, eyec, np.ones(LY)).reshape(ROWS, LX * SLOT)
    block = xf.reshape(2, GX, 2, 4, 2, MX)
    eyej = np.eye(per)
    tx = np.zeros((GX, 2, JS, per, 2, 4, SLOT), np.float32)
    tx[:, :, : 2 * per, :, :, :, :MX] = np.einsum("rahusk,ij->ahirjsuk", block, eyej).reshape(
        GX, 2, 2 * per, per, 2, 4, MX
    )
    tx = tx.reshape(GX * 2 * JS, per * 2 * 4 * SLOT)
    block = xi.reshape(2, MX, 2, GX, 2, 4)
    tix = np.zeros((GX, 2, JS, per, 2, 4, SLOT), np.float32)
    tix[:, :, : 2 * per, :, :, :, :MX] = np.einsum("rksahu,ij->ahisjruk", block, eyej).reshape(
        GX, 2, 2 * per, per, 2, 4, MX
    )
    tix = tix.reshape(GX * 2 * JS, per * 2 * 4 * SLOT)
    block = yi.reshape(2, 8, per, 2, GY, LY)
    tiy = np.zeros((LY, GY, 2, 8, JS), np.float32)
    tiy[..., : 2 * per] = np.einsum("rajsgy->ygsajr", block).reshape(LY, GY, 2, 8, 2 * per)
    tiy = tiy.reshape(LY * GY * 2, 8 * JS)
    zt_forward = zt_forward.reshape(GY, 2, 2, DEPTH).transpose(1, 0, 2, 3).reshape(2 * MODES, DEPTH)
    zt_inverse = zt_inverse.reshape(GY, 2, 2, DEPTH).transpose(1, 0, 2, 3).reshape(2, MODES, DEPTH)
    pair_pool = np.einsum("x,cC,yY->YCxcy", np.ones(2), np.eye(CH), np.repeat(np.eye(2), 2, 0))
    pair_pool = pair_pool.reshape(2 * CH, PAIR)
    lane_up = np.einsum("zZ,tT->ZTzt", np.repeat(np.eye(GRID_Z // 2), 2, 0), np.eye(STEPS))
    lane_up = lane_up.reshape(HALF, DEPTH)
    lane_pool = 0.125 * lane_up.T
    row_up = np.zeros((PAIR, 2, 24), np.float32)
    row_up[:, :, :CH] = pair_pool.T.reshape(PAIR, 2, CH)
    row_up = row_up.reshape(PAIR, 48)
    spread_o = np.einsum("x,oO,y->xoyO", np.ones(2), np.eye(CH), np.ones(LY)).reshape(PAIR, CH)
    same = np.einsum("xX,oc,yY->xoyXcY", np.eye(2), np.ones((CH, CH)), eyey).reshape(PAIR, PAIR)
    eyecc = np.eye(CH, dtype=np.float32)
    conv_place = np.zeros((3, 2, 128, 3, 4, CH), np.float32)
    for dx in range(3):
        for dy in range(3):
            for dz in range(3):
                for at in range(2):
                    conv_place[dz, at, 9 * dx + 3 * dy + dz, dx, dy + at] = 1.0
    conv_place = conv_place.reshape(6, 128, 12 * CH)
    conv_same = np.einsum("cC,o,d->coCd", eyecc, np.ones(24), np.ones(12))
    conv_same = conv_same.transpose(0, 1, 3, 2).reshape(24 * CH, 12 * CH)
    conv_sum = np.einsum("c,oO->ocO", np.ones(CH), np.eye(24)).reshape(24, 24 * CH)
    return [
        np.asarray(t, np.float32).astype(ml_dtypes.bfloat16)
        for t in (
            zt_forward,
            ty,
            gather,
            tx,
            tix,
            gather.T,
            tiy,
            zt_inverse,
            pair_pool,
            lane_pool,
            lane_up,
            row_up,
            spread_o,
            same,
            conv_place,
            conv_same,
            conv_sum,
        )
    ]


def mm(a, b):
    return jnp.dot(a, b, preferred_element_type=FLT)


def mm_nt(a, b):
    return lax.dot_general(a, b, (((1,), (1,)), ((), ())), preferred_element_type=FLT)


def mm_tn(a, b):
    return lax.dot_general(a, b, (((0,), (0,)), ((), ())), preferred_element_type=FLT)


def halves(value):
    high = value.astype(BF)
    return high, (value - high.astype(FLT)).astype(BF)


def kernel(*refs):
    (f_hbm, w_hbm, pw_hbm, bias_hbm, cw_hbm), refs = refs[:5], refs[5:]
    tables_hbm, refs = refs[:TABLES], refs[TABLES:]
    out_ref, refs = refs[0], refs[1:]
    (f_in, w_in, pw_in, bias_in, cw_in), refs = refs[:5], refs[5:]
    tables, refs = refs[:TABLES], refs[TABLES:]
    (
        f_rows,
        send_one,
        recv_one,
        send_two,
        recv_two,
        send_three,
        recv_three,
        send_four,
        recv_four,
        pool,
        point,
        taps,
        conv,
        w_wide,
        third,
        base,
        in_sem,
        table_sem,
        send_sem,
        recv_sem,
        halo_send,
        halo_recv,
        heard,
    ) = refs
    (
        t_zf,
        t_y,
        t_gather,
        t_x,
        t_ix,
        t_spread,
        t_iy,
        t_zi,
        t_pair_pool,
        t_lane_pool,
        t_lane_up,
        t_row_up,
        t_spread_o,
        t_same,
        t_conv_place,
        t_conv_same,
        t_conv_sum,
    ) = tables
    gx = lax.axis_index("gx")
    gy = lax.axis_index("gy")
    barrier = pltpu.get_barrier_semaphore()

    far = (2, 1, 3, 0)
    inner = lax.rem(gy, 4)
    lows = [lax.rem(inner + k, 4) for k in far]
    xs = [4 * lax.rem(lax.div(gx, 4) + k, 4) for k in far]

    planes = [4 * lax.rem(lax.div(gy, 4) + k, 8) for k in range(1, 8)]

    def each_gy(act):
        for step in (4, 3, 5, 2, 6, 1, 7):
            plane = planes[step - 1]
            for k in range(4):
                act(plane + lows[k])
        for k in range(3):
            act(gy - inner + lows[k])

    def each_gx(act):
        for k in far:
            y = lax.rem(lax.rem(gx, 4) + k, 4)
            for i in range(4 if k else 3):
                act(xs[i] + y)

    def greet(target):
        pl.semaphore_signal(barrier, inc=1, device_id=target, device_id_type=MESH)

    mine = [
        pltpu.make_async_copy(f_hbm, f_in, in_sem.at[0]),
        pltpu.make_async_copy(
            w_hbm.at[gx // 8, pl.ds(3 * lax.rem(gx, 8), 3)], w_in, in_sem.at[1]
        ),
        pltpu.make_async_copy(pw_hbm, pw_in, in_sem.at[2]),
        pltpu.make_async_copy(bias_hbm, bias_in, in_sem.at[3]),
        pltpu.make_async_copy(cw_hbm, cw_in, in_sem.at[4]),
    ]
    loads = [
        pltpu.make_async_copy(tables_hbm[i], tables[i], table_sem.at[i]) for i in range(TABLES)
    ]
    loads[0].start()
    mine[0].start()

    each_gy(lambda to: greet((gx, to)))
    at_y = lax.rem(gx, 4)
    x_mates = [xs[i] + at_y for i in range(3)]
    for mate in x_mates:
        greet((mate, gy))
    for k in (2, 1, 3):
        greet((gx - at_y + lax.rem(at_y + k, 4), gy))
    sides = [(dx, dy) for dx in (-1, 0, 1) for dy in (-1, 0, 1) if (dx, dy) != (0, 0)]

    def beside(dx, dy):
        return (lax.rem(gx + dx + GX, GX), lax.rem(gy + dy + GY, GY))

    for dx, dy in sides:
        if dx != 0 and dy != 0:
            greet(beside(dx, dy))
    for load in loads[1:]:
        load.start()
    for load in mine[1:]:
        load.start()

    mine[0].wait()
    loads[0].wait()
    f_rows[...] = f_in.reshape(ROWS, DEPTH)[...]
    hat = mm_nt(t_zf[...], f_rows[...]).astype(BF)
    for m in range(2):
        send_one[m] = hat[m * MODES : (m + 1) * MODES].reshape(GY, 2, ROWS)

    def along_gy(at, source, target):
        def send(to):
            pltpu.make_async_remote_copy(
                src_ref=source.at[to],
                dst_ref=target.at[gy],
                send_sem=send_sem.at[at],
                recv_sem=recv_sem.at[at],
                device_id=(gx, to),
                device_id_type=MESH,
            ).start()

        each_gy(send)
        pltpu.make_async_copy(source.at[gy], target.at[gy], recv_sem.at[at]).start()

    def arrived(at, whole):
        pltpu.make_async_copy(whole, whole, recv_sem.at[at]).wait()

    def left(at, source, count):
        part = source.at[pl.ds(0, count)]
        pltpu.make_async_copy(part, part, send_sem.at[at]).wait()

    pl.semaphore_wait(barrier, (GY - 1) + 6 + 4)
    for m in range(2):
        along_gy(m, send_one.at[m], recv_one.at[m])
    for mate in x_mates:
        pl.semaphore_signal(heard, inc=1, device_id=(mate, gy), device_id_type=MESH)

    def rim(which, dx, dy):
        sx = {-1: pl.ds(1, 1), 0: pl.ds(1, 4), 1: pl.ds(4, 1)}[dx]
        tx = {-1: pl.ds(5, 1), 0: pl.ds(1, 4), 1: pl.ds(0, 1)}[dx]
        sy = {-1: pl.ds(1, 1), 0: pl.ds(1, 2), 1: pl.ds(2, 1)}[dy]
        ty = {-1: pl.ds(3, 1), 0: pl.ds(1, 2), 1: pl.ds(0, 1)}[dy]
        return pltpu.make_async_remote_copy(
            src_ref=pool.at[sx, sy],
            dst_ref=pool.at[tx, ty],
            send_sem=halo_send.at[which],
            recv_sem=halo_recv.at[which],
            device_id=beside(dx, dy),
            device_id_type=MESH,
        )

    rims = [rim(i, dx, dy) for i, (dx, dy) in enumerate(sides)]

    w_wide[...] = jnp.zeros_like(w_wide)
    mine[1].wait()

    def widen(at, _):
        value = w_in.reshape(3 * CH, CH, 2, MX)[at].astype(FLT).reshape(2 * CH, MX)
        for u in range(4):
            w_wide[at, 0 : 2 * CH, u * SLOT : u * SLOT + MX] = value
        return 0

    lax.fori_loop(0, 3 * CH, widen, 0)

    for i in (1, 2):
        loads[i].wait()
    lane = lax.rem(lax.broadcasted_iota(jnp.int32, (8 * JS, ROWS), 1), LY)
    for m in range(2):
        arrived(m, recv_one.at[m])
        part = mm(t_y[...], recv_one[m].reshape(2 * GY, ROWS)).reshape(LY, 8 * JS, ROWS)
        chosen = part[0]
        for y in range(1, LY):
            chosen = jnp.where(lane == y, part[y], chosen)
        both = mm(jnp.concatenate(halves(chosen), axis=0), t_gather[...])
        second = both[: 8 * JS] + both[8 * JS :]
        second = [second[:, h * 128 : (h + 1) * 128].reshape(8, JS, 128) for h in range(2)]
        send_two[8 * m : 8 * m + 8] = jnp.concatenate(second, axis=1).astype(BF)

        if m == 0:
            pl.semaphore_wait(heard, 3)
        for k in far:
            y = lax.rem(lax.rem(gx, 4) + k, 4)
            for x in (2 * m, 2 * m + 1):
                to = 4 * x + y

                @pl.when(to != gx)
                def _(to=to):
                    pltpu.make_async_remote_copy(
                        src_ref=send_two.at[to],
                        dst_ref=recv_two.at[gx],
                        send_sem=send_sem.at[2],
                        recv_sem=recv_sem.at[2],
                        device_id=(to, gy),
                        device_id_type=MESH,
                    ).start()

    pltpu.make_async_copy(send_two.at[gx], recv_two.at[gx], recv_sem.at[2]).start()
    for i in (8, 9):
        loads[i].wait()
    for pair in range(LX // 2):
        rows = mm(t_pair_pool[...], f_rows[pair * PAIR : (pair + 1) * PAIR])
        high, low = halves(rows)
        cells = mm(high, t_lane_pool[...]) + mm(low, t_lane_pool[...])
        pool[pair + 1, 1:3] = cells.astype(BF).reshape(2, 9, 2, HALF)

    for copy in rims:
        copy.start()

    for i in (3, 4):
        loads[i].wait()
    arrived(2, recv_two)
    turned = mm_tn(recv_two[...].reshape(GX * 2 * JS, 128), t_x[...])
    group = lax.broadcasted_iota(jnp.int32, (SLOT, 128), 1) // SLOT
    for at in range(6):
        acc = jnp.zeros((SLOT, 128), FLT)
        for u in range(4):
            piece = turned[u * SLOT : (u + 1) * SLOT, at * 128 : (at + 1) * 128]
            acc = acc + jnp.where(group == u, piece, 0.0)
        acc = acc + pltpu.roll(acc, 64, 1)
        acc = acc + pltpu.roll(acc, 32, 1)
        third[at] = acc

    blocks = []
    for j in range(3):
        real = jnp.zeros((24, 128), FLT)
        imag = jnp.zeros((24, 128), FLT)
        for c in range(CH):
            w_real = w_wide[j * CH + c, pl.ds(0, 24, stride=2), :]
            w_imag = w_wide[j * CH + c, pl.ds(1, 24, stride=2), :]
            u_real = third[2 * j, c : c + 1, :]
            u_imag = third[2 * j + 1, c : c + 1, :]
            real = real + (w_real * u_real - w_imag * u_imag)
            imag = imag + (w_real * u_imag + w_imag * u_real)
        for value in (real, imag):
            tall = []
            for u in range(4):
                tall += [jnp.where(group[:24] == u, value, 0.0), jnp.zeros((8, 128), FLT)]
            blocks.append(jnp.concatenate(tall, axis=0).astype(BF))
    back = mm_nt(t_ix[...], jnp.concatenate(blocks, axis=1))
    send_three[...] = back.astype(BF).reshape(GX, 2 * JS, 128)
    at_three = 3 + lax.div(gx, 8)

    def send(to):
        pltpu.make_async_remote_copy(
            src_ref=send_three.at[to],
            dst_ref=recv_three.at[gx],
            send_sem=send_sem.at[3],
            recv_sem=recv_sem.at[at_three],
            device_id=(to, gy),
            device_id_type=MESH,
        ).start()

    each_gx(send)
    pltpu.make_async_copy(send_three.at[gx], recv_three.at[gx], recv_sem.at[at_three]).start()

    for i in (2, 3, 4):
        mine[i].wait()
    for i in range(10, TABLES):
        loads[i].wait()
    wide = mm_nt(t_spread_o[...], pw_in[...]).astype(BF)
    wide = mm_nt(wide, t_spread_o[...]).astype(BF)
    point[...] = wide * t_same[...]
    taps[...] = jnp.zeros_like(taps)
    for c in range(CH):
        taps[c, 0:CH, 0:27] = cw_in[c].astype(FLT)
    flat = taps[...].reshape(24 * CH, 128).astype(BF)
    for at in range(6):
        placed = mm(flat, t_conv_place[at]).astype(BF) * t_conv_same[...]
        conv[at * 24 : (at + 1) * 24] = mm(t_conv_sum[...], placed)

    for copy in rims:
        copy.wait_recv()

    @pl.when(gx == 0)
    def _():
        pool[0] = jnp.zeros((4, 9, 2, HALF), BF)

    @pl.when(gx == GX - 1)
    def _():
        pool[5] = jnp.zeros((4, 9, 2, HALF), BF)

    @pl.when(gy == 0)
    def _():
        pool[:, 0] = jnp.zeros((6, 9, 2, HALF), BF)

    @pl.when(gy == GY - 1)
    def _():
        pool[:, 3] = jnp.zeros((6, 9, 2, HALF), BF)

    for i in (5, 6, 7):
        loads[i].wait()
    for m in range(2):
        mine_three = recv_three.at[pl.ds(8 * m, 8)]
        arrived(3 + m, mine_three)
        wide_in = mine_three[...].astype(FLT)
        sides_in = [wide_in[:, h * JS : (h + 1) * JS].reshape(8 * JS, 128) for h in range(2)]
        spread = mm(jnp.concatenate(sides_in, axis=1).astype(BF), t_spread[...]).astype(BF)
        part = mm(t_iy[...], spread).reshape(LY, 2 * GY, ROWS)
        chosen = part[0]
        for y in range(1, LY):
            chosen = jnp.where(lane == y, part[y], chosen)
        send_four[m] = chosen.astype(BF).reshape(GY, 2, ROWS)
        along_gy(5 + m, send_four.at[m], recv_four.at[m])

    column = jnp.sum(t_spread_o[...].astype(FLT) * bias_in[...], axis=1, keepdims=True)
    spot = lax.broadcasted_iota(jnp.int32, (48, HALF), 1)
    conv_matrix = conv[...].astype(BF)
    for pair in range(LX // 2):
        sums = mm(conv_matrix, pool[pair : pair + 3].reshape(12 * CH, HALF))
        below = jnp.where(spot >= STEPS, pltpu.roll(sums[0:48], STEPS, 1), 0.0)
        above = jnp.where(spot < HALF - STEPS, pltpu.roll(sums[96:144], HALF - STEPS, 1), 0.0)
        high, low = halves(jax.nn.gelu(sums[48:96] + below + above))
        span = slice(pair * PAIR, (pair + 1) * PAIR)
        up = mm(t_row_up[...], mm(high, t_lane_up[...]).astype(BF))
        up = up + mm(t_row_up[...], mm(low, t_lane_up[...]).astype(BF))
        base[span] = mm(point[...], f_rows[span]) + up + column

    arrived(5, recv_four.at[0])
    columns = recv_four[0].reshape(2 * GY, ROWS).astype(FLT).T.astype(BF)
    for pair in range(LX // 2):
        span = slice(pair * PAIR, (pair + 1) * PAIR)
        base[span] += mm(columns[span], t_zi[0])
    arrived(6, recv_four.at[1])
    columns = recv_four[1].reshape(2 * GY, ROWS).astype(FLT).T.astype(BF)
    for pair in range(LX // 2):
        span = slice(pair * PAIR, (pair + 1) * PAIR)
        total = mm(columns[span], t_zi[1]) + base[span]
        out_ref[pair * 36 : (pair + 1) * 36] = jax.nn.gelu(total).astype(BF).reshape(36, 4, DEPTH)
    for m in range(2):
        left(m, send_one.at[m], GY - 1)
        left(5 + m, send_four.at[m], GY - 1)
    left(2, send_two, GX - 1)
    left(3, send_three, GX - 1)
    for copy in rims:
        copy.wait_send()


def local(features, mode_weights, point_weight, bias_term, conv_weight):
    tables = make_tables()
    f = features.transpose(0, 2, 1, 3).reshape(LX * CH, LY, DEPTH)
    w = mode_weights.transpose(0, 1, 3, 4, 2, 5)
    taps = conv_weight.transpose(1, 2, 0)
    operands = [f, w, point_weight, bias_term.reshape(1, CH), taps]
    vmem = [
        pltpu.VMEM(f.shape, BF),
        pltpu.VMEM((3,) + w.shape[2:], BF),
        pltpu.VMEM(point_weight.shape, BF),
        pltpu.VMEM((1, CH), FLT),
        pltpu.VMEM(taps.shape, BF),
    ]
    vmem += [pltpu.VMEM(t.shape, BF) for t in tables]
    vmem += [
        pltpu.VMEM((ROWS, DEPTH), BF),
        pltpu.VMEM((2, GY, 2, ROWS), BF),
        pltpu.VMEM((2, GY, 2, ROWS), BF),
        pltpu.VMEM((GX, 2 * JS, 128), BF),
        pltpu.VMEM((GX, 2 * JS, 128), BF),
        pltpu.VMEM((GX, 2 * JS, 128), BF),
        pltpu.VMEM((GX, 2 * JS, 128), BF),
        pltpu.VMEM((2, GY, 2, ROWS), BF),
        pltpu.VMEM((2, GY, 2, ROWS), BF),
        pltpu.VMEM((6, 4, 9, 2, HALF), BF),
        pltpu.VMEM((PAIR, PAIR), BF),
        pltpu.VMEM((CH, 24, 128), FLT),
        pltpu.VMEM((144, 12 * CH), FLT),
        pltpu.VMEM((3 * CH, 48, 128), FLT),
        pltpu.VMEM((6, SLOT, 128), FLT),
        pltpu.VMEM((ROWS, DEPTH), FLT),
        pltpu.SemaphoreType.DMA((5,)),
        pltpu.SemaphoreType.DMA((TABLES,)),
        pltpu.SemaphoreType.DMA((7,)),
        pltpu.SemaphoreType.DMA((7,)),
        pltpu.SemaphoreType.DMA((8,)),
        pltpu.SemaphoreType.DMA((8,)),
        pltpu.SemaphoreType.REGULAR,
    ]
    out = pl.pallas_call(
        kernel,
        out_shape=jax.ShapeDtypeStruct(f.shape, BF),
        in_specs=[pl.BlockSpec(memory_space=pltpu.HBM)] * (5 + len(tables)),
        out_specs=pl.BlockSpec(memory_space=pltpu.VMEM),
        scratch_shapes=vmem,
        compiler_params=pltpu.CompilerParams(
            collective_id=0, has_side_effects=True, vmem_limit_bytes=48 << 20
        ),
        name="layer",
    )(*[pltpu.with_memory_space_constraint(t, pltpu.HBM) for t in operands + [jnp.asarray(t) for t in tables]])
    return out.reshape(LX, CH, LY, DEPTH).transpose(0, 2, 1, 3)


def solution(mesh):
    in_specs = (P("gx", "gy", None, None), P("gy", None, None, None, None, None), P(), P(), P())
    out_specs = P("gx", "gy", None, None)
    return jax.shard_map(local, mesh=mesh, in_specs=in_specs, out_specs=out_specs, check_vma=False)
```
